256 devices in a mesh: dom: 64 (over z_hi, y, x), rep: 4 (over z_lo, core).
Axes of the slice: x: 4, y: 4, z: 8 (z_hi: 4, z_lo: 2; z = z_hi * 2 + z_lo), core: 2. Of those that a mesh axis runs over, the one named last changes fastest.
Arguments:
- entity_slab: bfloat16 [262144, 400], P('dom'), may hold values from -1.796875 to 1.796875
- entity_state: float32 [262144], P(('dom', 'rep')), may hold values from 0.02 to 0.2
- relation_diag: float32 [1345, 400], replicated, may hold values from -4 to 4
- relation_state: float32 [1345], replicated, may hold values from 0.05 to 0.5
- edge_source: int32 [1048576], P(('dom', 'rep')), may hold values from 0 to 4095
- edge_target: int32 [1048576], P(('dom', 'rep')), may hold values from 0 to 4095
- edge_relation: int32 [1048576], P(('dom', 'rep')), may hold values from 0 to 1344
- edge_count: int32 [256], P(('dom', 'rep')), may hold values from 1 to 4096, 524288 in all
- negatives: int32 [65536], P('dom'), may hold values from 0 to 4095
Outputs:
- new_slab: bfloat16 [262144, 400], P(('dom', 'rep'))
- new_state: float32 [262144], P(('dom', 'rep'))
- new_relation: float32 [1345, 400], replicated
- new_relation_state: float32 [1345], replicated
The draws below stay inside these ranges and needn't reach their ends.
Inputs may be any that keep to these rules, and one draw needn't show every extreme that they name: `edge_count`: a device's count; some device has exactly 4096 live slots.
All inputs are finite; a program needn't handle non-finite values.
Results may differ from the reference program's by a relative error of at most 0.003.
Values may be sent and summed in bfloat16 or wider, within the bound.
No kernel may reach another device: no remote copies, remote signals or barrier semaphores. Data moves between devices by JAX's collectives and lax.ppermute only.
A program may use at most 128 MiB of HBM per device.

```python
import math
import jax
import jax.numpy as jnp
import numpy as np
from jax import lax

DIM = 400
NEG = 1024
NREL = 1345
ENT_PART = 4096
EDGES_DEV = 4096
ENT_TOTAL = 262144
N_DOM = 64
N_REP = 4
DEVICES = 256


def place_ends(array, stream_key, smallest, largest):
    extent = array.shape
    place = [jax.random.randint(jax.random.fold_in(stream_key, axis), (), 0, extent[axis]) for axis in range(len(extent))]
    array = array.at[tuple(place)].set(smallest)
    longest = extent.index(max(extent))
    place[longest] = (place[longest] + 1) % extent[longest]
    return array.at[tuple(place)].set(largest)


def levels(rng, shape, cuts, smallest, top_value):
    loudness, own = 1.0, jax.random.fold_in(rng, 6)
    for dim, shards_of in cuts:
        steps = jnp.exp(jax.random.uniform(jax.random.fold_in(own, dim), (shards_of,), jnp.float32, smallest / len(cuts), top_value / len(cuts)))
        loudness = loudness * jnp.repeat(steps, shape[dim] // shards_of).reshape([-1 if axis == dim else 1 for axis in range(len(shape))])
    return loudness


def profile(count, total, bound, skew):
    loads = [(1 << 20) // math.isqrt(standing ** skew) + 1 for standing in range(2, count + 1)]
    rest, counts = total - bound - (count - 1), [1] * (count - 1)
    while rest > 0:
        movable = [i for i in range(count - 1) if counts[i] < bound]
        whole, left = sum([loads[i] for i in movable]), rest
        for i in movable:
            more = min(bound - counts[i], max(1, left * loads[i] // whole), rest)
            counts[i] = counts[i] + more
            rest = rest - more
    return np.array([bound] + counts)


def ragged_sizes(own_key, count, total, limit, slope):
    if count == 2:
        one = jax.random.randint(own_key, (), max(1, total - limit), min(limit, total - 1) + 1)
        return jnp.stack([one, total - one])
    sizes = jnp.asarray(profile(count, total, limit, slope), jnp.int32)
    pairs = (count - 1) // 2
    source_of, receiver = sizes[1:1 + 2 * pairs:2], sizes[2:2 + 2 * pairs:2]
    slack = jnp.minimum(source_of - 1, limit - receiver)
    passed = jax.random.randint(jax.random.fold_in(own_key, 1), (pairs,), 0, 1 << 20) % (slack + 1)
    sizes = sizes.at[1:1 + 2 * pairs:2].set(source_of - passed).at[2:2 + 2 * pairs:2].set(receiver + passed)
    return sizes[jax.random.permutation(jax.random.fold_in(own_key, 2), count)]


def gaussian(key, shape, deviation, reach, shards=(), kind=jnp.bfloat16):
    level = levels(key, shape, shards, -0.22, 0.18) if shards else 1.0
    drawn = jax.random.normal(key, shape, jnp.float32) * deviation * level
    return jnp.minimum(jnp.maximum(drawn, -reach), reach).astype(kind)


def setup_inputs(seed: int = 0) -> dict:
    streams_of = jax.random.split(jax.random.key(seed), 10)
    return {
        "entity_slab": gaussian(streams_of[0], (ENT_TOTAL, DIM), 0.45, 1.796875, ((0, 64),)),
        "entity_state": jnp.clip(jnp.exp(math.log(0.2) - 2.3025851 * jax.random.uniform(streams_of[1], (ENT_TOTAL,), jnp.float32) ** levels(streams_of[1], (ENT_TOTAL,), ((0, 256),), -0.2, 0.2)), 0.02, 0.2),
        "relation_diag": gaussian(streams_of[2], (NREL, DIM), 1.0, 4.0, (), jnp.float32),
        "relation_state": jnp.clip(jnp.exp(jax.random.uniform(streams_of[3], (NREL,), jnp.float32, math.log(0.05), math.log(0.5))), 0.05, 0.5),
        "edge_source": place_ends(jax.random.randint(streams_of[4], (DEVICES * EDGES_DEV,), 0, ENT_PART), jax.random.fold_in(streams_of[4], 1), 0, ENT_PART - 1).astype(jnp.int32),
        "edge_target": place_ends(jax.random.randint(streams_of[5], (DEVICES * EDGES_DEV,), 0, ENT_PART), jax.random.fold_in(streams_of[5], 1), 0, ENT_PART - 1).astype(jnp.int32),
        "edge_relation": place_ends(jax.random.randint(streams_of[6], (DEVICES * EDGES_DEV,), 0, NREL), jax.random.fold_in(streams_of[6], 1), 0, NREL - 1).astype(jnp.int32),
        "edge_count": ragged_sizes(streams_of[7], DEVICES, DEVICES * EDGES_DEV // 2, EDGES_DEV, 2).astype(jnp.int32),
        "negatives": place_ends(jax.random.randint(streams_of[8], (N_DOM * NEG,), 0, ENT_PART), jax.random.fold_in(streams_of[8], 1), 0, ENT_PART - 1).astype(jnp.int32),
    }


def score_edges(s_rows, t_rows, r_rows, negative_rows, valid):
    source = s_rows.astype(jnp.float32)
    target = t_rows.astype(jnp.float32)
    lifted = source * r_rows
    pos = lax.optimization_barrier(jnp.sum(lifted * target, axis=1))
    lifted_b = lifted.astype(jnp.bfloat16)
    neg = lax.dot_general(lifted_b, negative_rows, (((1,), (1,)), ((), ())), preferred_element_type=jnp.float32)
    gpos = -jax.nn.sigmoid(-pos) * valid
    gneg = (jax.nn.sigmoid(neg) * (valid[:, None] / neg.shape[1])).astype(jnp.bfloat16)
    grad_u = gpos[:, None] * target + jnp.dot(gneg, negative_rows, preferred_element_type=jnp.float32)
    grad_t = gpos[:, None] * lifted
    grad_n = lax.dot_general(gneg, lifted_b, (((0,), (0,)), ((), ())), preferred_element_type=jnp.float32)
    return (grad_u * r_rows, grad_t, grad_u * source, grad_n)

def reference(entity_slab, entity_state, relation_diag, relation_state, edge_source, edge_target, edge_relation, edge_count, negatives):
    sources = edge_source.reshape(DEVICES, EDGES_DEV)
    targets = edge_target.reshape(DEVICES, EDGES_DEV)
    relations = edge_relation.reshape(DEVICES, EDGES_DEV)
    negs = negatives.reshape(N_DOM, NEG)
    slots = jnp.arange(EDGES_DEV, dtype=jnp.int32)

    def visit(carry, item):
        grads, rel_grad = carry
        src, dst, rel, count, device = item
        part = (device // N_REP).astype(jnp.int32)
        other = jnp.bitwise_xor(part, jnp.int32(N_DOM // 2)).astype(jnp.int32)
        valid = (slots < count).astype(jnp.float32)
        neg_idx = lax.dynamic_index_in_dim(negs, part, 0, keepdims=False)
        src_g = part * ENT_PART + src
        dst_g = other * ENT_PART + dst
        neg_g = other * ENT_PART + neg_idx
        grad_s, grad_t, grad_r, grad_n = score_edges(entity_slab[src_g], entity_slab[dst_g], relation_diag[rel], entity_slab[neg_g], valid)
        grads = grads.at[src_g].add(grad_s).at[dst_g].add(grad_t).at[neg_g].add(grad_n)
        rel_grad = rel_grad.at[rel].add(grad_r)
        return ((grads, rel_grad), None)
    init = (jnp.zeros((ENT_TOTAL, DIM), jnp.float32), jnp.zeros((NREL, DIM), jnp.float32))
    (grads, rel_grad), _ = lax.scan(visit, init, (sources, targets, relations, edge_count, jnp.arange(DEVICES, dtype=jnp.int32)))
    new_state = entity_state + lax.optimization_barrier(jnp.mean(grads * grads, axis=1))
    new_slab = (entity_slab.astype(jnp.float32) - 0.1 * grads / jnp.sqrt(new_state)[:, None]).astype(jnp.bfloat16)
    new_relation_state = relation_state + lax.optimization_barrier(jnp.mean(rel_grad * rel_grad, axis=1))
    new_relation = relation_diag - 0.1 * rel_grad / jnp.sqrt(new_relation_state)[:, None]
    return (new_slab, new_state, new_relation, new_relation_state)
```

```python
import functools

import jax
import jax.numpy as jnp
from jax import lax
from jax.experimental import pallas as pl
from jax.experimental.pallas import tpu as pltpu
from jax.sharding import PartitionSpec as P

BLOCK = 512
LANES = 128
SUBLANES = 8
VMEM_BYTES = 56 << 20
RATE = 0.1
BF16, F32, I32 = jnp.bfloat16, jnp.float32, jnp.int32


def swapped(x, axis, mask):
    return lax.ppermute(x, axis, [(i, i ^ mask) for i in range(lax.axis_size(axis))])


def swapped_far(x, dom_mask, rep_mask):
    doms, reps = lax.axis_size("dom"), lax.axis_size("rep")
    pairs = [
        (d * reps + r, (d ^ dom_mask) * reps + (r ^ rep_mask))
        for d in range(doms)
        for r in range(reps)
    ]
    return lax.ppermute(x, ("dom", "rep"), pairs)


def one_hot(idx, base, rows):
    row = lax.broadcasted_iota(I32, (rows, idx.shape[1]), 0)
    return jnp.where(row == idx - base, 1.0, 0.0).astype(BF16)


def mm(a, b):
    return jnp.dot(a, b, preferred_element_type=F32)


def mm_nt(a, b):
    return lax.dot_general(a, b, (((1,), (1,)), ((), ())), preferred_element_type=F32)


def call(kernel, name, grid, in_specs, out_specs, out_shape, scratch, flops, *args):
    moved = sum(a.size * a.dtype.itemsize for a in args)
    moved += sum(o.size * o.dtype.itemsize for o in jax.tree.leaves(out_shape))
    return pl.pallas_call(
        kernel,
        grid_spec=pltpu.PrefetchScalarGridSpec(
            num_scalar_prefetch=1,
            grid=(grid,),
            in_specs=in_specs,
            out_specs=out_specs,
            scratch_shapes=scratch,
        ),
        out_shape=out_shape,
        compiler_params=pltpu.CompilerParams(vmem_limit_bytes=VMEM_BYTES),
        cost_estimate=pl.CostEstimate(flops=flops, bytes_accessed=moved, transcendentals=0),
        name=name,
    )(*args)


def whole(shape):
    return pl.BlockSpec(shape, lambda i, c: (0,) * len(shape))


def edge_block(rows):
    return pl.BlockSpec((rows, BLOCK), lambda i, c: (0, i))


def live(scal):
    return pl.program_id(0) * BLOCK < scal[0]


def gather_kernel(order, scal, idx_ref, *refs):
    tables, out_ref = refs[:-1], refs[-1]

    @pl.when(live(scal))
    def _():
        idx = idx_ref[...]
        out_ref[...] = gathered(order, scal, idx, tables).astype(out_ref.dtype)


def gathered(order, scal, idx, tables):
    total = None
    for apart, table in zip(order, tables, strict=True):
        rows = table.shape[1]
        base = apart * rows if isinstance(scal, int) else (scal[1] ^ apart) * rows
        y = mm(table[...], one_hot(idx, base, rows))
        total = y if total is None else total + y
    return total


def own_gather_kernel(scal, idx_ref, table_ref, out_ref):
    @pl.when(live(scal))
    def _():
        idx, chunk = idx_ref[...], 1024
        total = None
        for base in range(0, table_ref.shape[1], chunk):
            y = mm(table_ref[:, base : base + chunk], one_hot(idx, base, chunk))
            total = y if total is None else total + y
        out_ref[...] = total.astype(out_ref.dtype)


def relation_gather_kernel(scal, idx_ref, table_ref, out_ref):
    @pl.when(live(scal))
    def _():
        both = mm(table_ref[...], one_hot(idx_ref[...], 0, table_ref.shape[1]))
        half = both.shape[0] // 2
        out_ref[...] = both[:half] + both[half:]


def edge_kernel(
    order,
    scal,
    s_ref,
    r_ref,
    t_idx_ref,
    r_idx_ref,
    neg_t_ref,
    neg_ref,
    *refs,
):
    tables = refs[: len(order)]
    gs_ref, gt_ref, rel_ref, gn_ref, rel_acc, gn_acc = refs[len(order) :]
    i = pl.program_id(0)

    @pl.when(i == 0)
    def _():
        rel_acc[...] = jnp.zeros_like(rel_acc)
        gn_acc[...] = jnp.zeros_like(gn_acc)

    @pl.when(live(scal))
    def _():
        t = gathered(order, scal, t_idx_ref[...], tables)
        s = s_ref[...].astype(F32)
        r = r_ref[...]
        u = s * r
        ub = u.astype(BF16)
        lane = lax.broadcasted_iota(I32, (1, BLOCK), 1) + i * BLOCK
        valid = jnp.where(lane < scal[0], 1.0, 0.0)
        pos = jnp.sum(u * t, axis=0, keepdims=True)
        gpos = -jax.nn.sigmoid(-pos) * valid
        neg = mm(neg_ref[...], ub)
        gneg = (jax.nn.sigmoid(neg) * (valid * (1.0 / neg.shape[0]))).astype(BF16)
        gu = gpos * t + mm(neg_t_ref[...], gneg)
        gs_ref[...] = (gu * r).astype(BF16)
        gt_ref[...] = (gpos * u).astype(BF16)
        gn_acc[...] += mm_nt(ub, gneg)
        hot = one_hot(r_idx_ref[...], 0, rel_acc.shape[1])
        rel_acc[...] += mm_nt((gu * s).astype(BF16), hot)

    @pl.when(i == pl.num_programs(0) - 1)
    def _():
        gn_ref[...] = gn_acc[...].astype(BF16)
        for part, cell, slot, rows, cols in tiles(rel_ref.shape, rel_acc.shape):
            to = (part ^ scal[1], cell ^ (scal[2] & 15), pl.ds(slot * SUBLANES, SUBLANES))
            if rows is None:
                rel_ref[to] = jnp.zeros((SUBLANES, LANES), F32)
            else:
                rel_ref[to] = rel_acc[rows, cols]


def tiles(packed, flat):
    parts, cells, rows, _ = packed
    slots = rows // SUBLANES
    wide = flat[1] // parts // LANES
    for part in range(parts):
        for cell in range(cells):
            for slot in range(slots):
                tile = cell * slots + slot
                row, col = divmod(tile, wide)
                if row * SUBLANES >= flat[0]:
                    yield part, cell, slot, None, None
                else:
                    col = (part * wide + col) * LANES
                    yield (
                        part,
                        cell,
                        slot,
                        slice(row * SUBLANES, (row + 1) * SUBLANES),
                        slice(col, col + LANES),
                    )


def scatter_kernel(with_neg, scal, g_ref, idx_ref, *refs):
    if with_neg:
        gn_ref, n_idx_ref, *refs = refs
    keep_ref, send_ref, acc = refs
    i = pl.program_id(0)
    parts, _, rows = acc.shape

    @pl.when(i == 0)
    def _():
        for apart in range(parts):
            if not with_neg:
                acc[apart] = jnp.zeros(acc.shape[1:], F32)
                continue
            base = (scal[1] ^ apart) * rows
            acc[apart] = mm_nt(gn_ref[...], one_hot(n_idx_ref[...], base, rows))

    @pl.when(live(scal))
    def _():
        idx = idx_ref[...]
        for apart in range(parts):
            base = (scal[1] ^ apart) * rows
            acc[apart] += mm_nt(g_ref[...], one_hot(idx, base, rows))

    @pl.when(i == pl.num_programs(0) - 1)
    def _():
        for apart in range(0, parts, 2):
            keep_ref[apart // 2] = acc[apart]
            send_ref[apart // 2] = acc[apart + 1].astype(BF16)


def scatter(name, scal, g, idx, parts, rows, *neg):
    width, edges = g.shape
    half = (parts // 2, width, rows)
    return call(
        functools.partial(scatter_kernel, bool(neg)),
        name,
        edges // BLOCK,
        [edge_block(width), edge_block(1)] + [whole(x.shape) for x in neg],
        [whole(half), whole(half)],
        [jax.ShapeDtypeStruct(half, F32), jax.ShapeDtypeStruct(half, BF16)],
        [pltpu.VMEM((parts, width, rows), F32)],
        2 * width * parts * rows * edges,
        scal,
        g,
        idx,
        *neg,
    )


def relation_update_kernel(scal, rel_ref, state_ref, *refs):
    g_refs, (new_rel_ref, new_state_ref, flat) = refs[:-3], refs[-3:]
    cells, rows = 16, g_refs[0].shape[2]
    rep = scal[1]
    for k, g_ref in enumerate(g_refs):
        for cell in range(cells):
            away = cell ^ (scal[2] & 15)
            flat[rep ^ k, cell] = g_ref[away & 3, away >> 2].astype(F32)
    parts = len(g_refs)
    wide = 3
    packed = (parts, cells, rows, LANES)
    width, count = rel_ref.shape
    pieces = {}
    for part, cell, slot, trows, tcols in tiles(packed, (width, parts * wide * LANES)):
        if trows is not None:
            pieces[trows.start, tcols.start] = (part, cell, slot)
    for col in range(0, count, LANES):
        n = min(LANES, count - col)
        total = jnp.zeros((1, LANES), F32)
        square = jnp.zeros((SUBLANES, LANES), F32)
        for row in range(0, width, SUBLANES):
            part, cell, slot = pieces[row, col]
            g = flat[part, cell, slot * SUBLANES : (slot + 1) * SUBLANES]
            square = square + g * g
        total = jnp.sum(square, axis=0, keepdims=True) * (1.0 / width)
        state = state_ref[:, col : col + n] + total[:, :n]
        new_state_ref[:, col : col + n] = state
        scale = RATE / jnp.sqrt(state)
        for row in range(0, width, SUBLANES):
            part, cell, slot = pieces[row, col]
            g = flat[part, cell, slot * SUBLANES : (slot + 1) * SUBLANES]
            at = (slice(row, row + SUBLANES), slice(col, col + n))
            new_rel_ref[at] = rel_ref[at] - g[:, :n] * scale


def body(
    entity_slab,
    entity_state,
    relation_diag,
    relation_state,
    edge_source,
    edge_target,
    edge_relation,
    edge_count,
    negatives,
):
    slab = entity_slab.T
    relations = relation_diag.T
    width, rows_part = slab.shape
    reps = lax.axis_size("rep")
    half = lax.axis_size("dom") // 2
    quarter = rows_part // reps
    rep, dom = lax.axis_index("rep"), lax.axis_index("dom")
    edges, n_neg, n_rel = edge_source.shape[0], negatives.shape[0], relation_diag.shape[0]
    scal = jnp.stack([edge_count[0], rep.astype(I32), dom.astype(I32)])
    all_neg = jnp.stack([jnp.int32(n_neg), rep.astype(I32), dom.astype(I32)])
    src, dst, rel = (x.reshape(1, edges) for x in (edge_source, edge_target, edge_relation))
    neg_idx = negatives.reshape(1, n_neg)

    own = lax.dynamic_slice_in_dim(slab, rep * quarter, quarter, 1)
    far = swapped_far(own, half, 2)
    near = swapped(far, "rep", 2)
    far_core = swapped(far, "rep", 1)
    near_core = swapped(near, "rep", 1)
    order = (2, 0, 3, 1)
    tables = (far, near, far_core, near_core)

    s_rows = call(
        own_gather_kernel,
        "source_rows",
        edges // BLOCK,
        [edge_block(1), whole(slab.shape)],
        edge_block(width),
        jax.ShapeDtypeStruct((width, edges), BF16),
        [],
        2 * width * rows_part * edges,
        scal,
        src,
        slab,
    )
    wide = -(-n_rel // (reps * LANES)) * reps * LANES
    padded = jnp.pad(relations, ((0, 0), (0, wide - n_rel)))
    high = padded.astype(BF16)
    low = (padded - high.astype(F32)).astype(BF16)
    split = jnp.concatenate([high, low], axis=0)
    r_rows = call(
        relation_gather_kernel,
        "relation_rows",
        edges // BLOCK,
        [edge_block(1), whole(split.shape)],
        edge_block(width),
        jax.ShapeDtypeStruct((width, edges), F32),
        [],
        4 * width * wide * edges,
        scal,
        rel,
        split,
    )
    neg_t = call(
        functools.partial(gather_kernel, order),
        "negative_rows",
        n_neg // BLOCK,
        [edge_block(1)] + [whole(t.shape) for t in tables],
        edge_block(width),
        jax.ShapeDtypeStruct((width, n_neg), BF16),
        [],
        2 * width * rows_part * n_neg,
        all_neg,
        neg_idx,
        *tables,
    )
    cells = 16
    slots = -(-(width // SUBLANES * wide // reps // LANES) // cells)
    packed = (reps, cells, slots * SUBLANES, LANES)
    grad_s, grad_t, grad_r, grad_n = call(
        functools.partial(edge_kernel, order),
        "edges",
        edges // BLOCK,
        [
            edge_block(width),
            edge_block(width),
            edge_block(1),
            edge_block(1),
            whole((width, n_neg)),
            whole((n_neg, width)),
        ]
        + [whole(t.shape) for t in tables],
        [edge_block(width), edge_block(width), whole(packed), whole((width, n_neg))],
        [
            jax.ShapeDtypeStruct((width, edges), BF16),
            jax.ShapeDtypeStruct((width, edges), BF16),
            jax.ShapeDtypeStruct(packed, F32),
            jax.ShapeDtypeStruct((width, n_neg), BF16),
        ],
        [pltpu.VMEM((width, wide), F32), pltpu.VMEM((width, n_neg), F32)],
        2 * width * edges * (rows_part + 3 * n_neg + wide),
        scal,
        s_rows,
        r_rows,
        dst,
        rel,
        neg_t,
        neg_t.T,
        *tables,
    )

    apart = grad_r.reshape(2, 2, *packed[1:])
    pair = apart[:, 0] + swapped(apart[:, 1], "rep", 1)
    grid = (pair[0] + swapped(pair[1], "rep", 2)).reshape(4, 4, *packed[2:])
    line = (grid[:, 0] + swapped(grid[:, 1], "dom", 1)) + (
        swapped(grid[:, 2], "dom", 2) + swapped(grid[:, 3], "dom", 3)
    )
    cell = (line[0] + swapped(line[1], "dom", 4)) + (
        swapped(line[2], "dom", 8) + swapped(line[3], "dom", 12)
    )
    total = (cell + swapped(cell, "dom", 16)) + (
        swapped(cell, "dom", 32) + swapped(cell, "dom", 48)
    )
    total = total.astype(BF16)
    line = jnp.stack([total] + [swapped(total, "dom", 4 * k) for k in (1, 2, 3)])
    grid = jnp.stack([line] + [swapped(line, "dom", k) for k in (1, 2, 3)])
    other = swapped(grid, "rep", 2)
    grad_rel = (grid, swapped(grid, "rep", 1), other, swapped(other, "rep", 1))

    dst_keep, dst_send = scatter(
        "target_grads", scal, grad_t, dst, reps, quarter, grad_n, neg_idx
    )
    src_keep, src_send = scatter("source_grads", scal, grad_s, src, reps, quarter)
    got = dst_keep + swapped(dst_send, "rep", 1).astype(F32)
    got = got[1] + swapped(got[0].astype(BF16), "rep", 2).astype(F32)
    returned = swapped_far(got.astype(BF16), half, 2)
    kept = src_keep + swapped(src_send, "rep", 1).astype(F32)
    kept = kept[0] + swapped(kept[1].astype(BF16), "rep", 2).astype(F32)
    grads = kept + returned.astype(F32)

    new_state = entity_state + jnp.mean(grads * grads, axis=0)
    new_slab = (own.astype(F32) - RATE * grads / jnp.sqrt(new_state)[None, :]).astype(BF16)
    new_relation, new_relation_state = call(
        relation_update_kernel,
        "relation_update",
        1,
        [whole((width, n_rel)), whole((1, n_rel))] + [whole(g.shape) for g in grad_rel],
        [whole((width, n_rel)), whole((1, n_rel))],
        [jax.ShapeDtypeStruct((width, n_rel), F32), jax.ShapeDtypeStruct((1, n_rel), F32)],
        [pltpu.VMEM((reps, cells, packed[2], LANES), F32)],
        width * n_rel * 8,
        scal,
        relations,
        relation_state.reshape(1, n_rel),
        *grad_rel,
    )
    return (new_slab.T, new_state, new_relation.T, new_relation_state.reshape(n_rel))


def solution(mesh):
    in_specs = (
        P("dom", None),
        P(("dom", "rep")),
        P(),
        P(),
        P(("dom", "rep")),
        P(("dom", "rep")),
        P(("dom", "rep")),
        P(("dom", "rep")),
        P("dom"),
    )
    out_specs = (P(("dom", "rep"), None), P(("dom", "rep")), P(), P())
    return jax.shard_map(body, mesh=mesh, in_specs=in_specs, out_specs=out_specs, check_vma=False)
```

```python
import functools

import jax
import jax.numpy as jnp
from jax import lax
from jax.experimental import pallas as pl
from jax.experimental.pallas import tpu as pltpu
from jax.sharding import PartitionSpec as P

BLOCK = 512
FINE = 256
WIDE = 1024
WINDOW = 1280
LANES = 128
SUBLANES = 8
PIECES = 2
RETURNS = 2
VMEM_BYTES = 56 << 20
RATE = 0.1
BF16, F32, I32 = jnp.bfloat16, jnp.float32, jnp.int32


def swapped(x, axis, mask):
    return lax.ppermute(x, axis, [(i, i ^ mask) for i in range(lax.axis_size(axis))])


def swapped_far(x, dom_mask, rep_mask):
    doms, reps = lax.axis_size("dom"), lax.axis_size("rep")
    pairs = [
        (d * reps + r, (d ^ dom_mask) * reps + (r ^ rep_mask))
        for d in range(doms)
        for r in range(reps)
    ]
    return lax.ppermute(x, ("dom", "rep"), pairs)


def one_hot(idx, base, rows):
    row = lax.broadcasted_iota(I32, (rows, idx.shape[1]), 0)
    return jnp.where(row == idx - base, 1.0, 0.0).astype(BF16)


def mm(a, b):
    return jnp.dot(a, b, preferred_element_type=F32)


def mm_nt(a, b):
    return lax.dot_general(a, b, (((1,), (1,)), ((), ())), preferred_element_type=F32)


def call(kernel, name, grid, in_specs, out_specs, out_shape, scratch, *args):
    return pl.pallas_call(
        kernel,
        grid_spec=pltpu.PrefetchScalarGridSpec(
            num_scalar_prefetch=1,
            grid=(grid,),
            in_specs=in_specs,
            out_specs=out_specs,
            scratch_shapes=scratch,
        ),
        out_shape=out_shape,
        compiler_params=pltpu.CompilerParams(vmem_limit_bytes=VMEM_BYTES),
        cost_estimate=pl.CostEstimate(flops=0, bytes_accessed=0, transcendentals=0),
        name=name,
    )(*args)


def whole(shape):
    return pl.BlockSpec(shape, lambda i, c: (0,) * len(shape))


def edge_block(rows, block=BLOCK):
    return pl.BlockSpec((rows, block), lambda i, c: (0, i))


def live(scal, block=BLOCK):
    return pl.program_id(0) * block < scal[0]


def span(scal, which, block):
    each = block // FINE
    at = 3 + which
    first, last = None, None
    for k in range(each):
        cell = at + 4 * (pl.program_id(0) * each + k)
        low, high = scal[cell], scal[cell + 1]
        first = low if first is None else jnp.minimum(first, low)
        last = high if last is None else jnp.maximum(last, high)
    return first, last


def meets(spanned, base, rows):
    return (spanned[0] < base + rows) & (spanned[1] >= base)


def table_rows(idx, pieces):
    total = None
    for base, piece in pieces:
        y = mm(piece, one_hot(idx, base, piece.shape[1]))
        total = y if total is None else total + y
    return total


def over_windows(scal, rows, idx_ref, visit):
    cells = []
    for k in range(WIDE // FINE):
        at = 3 + 4 * (pl.program_id(0) * (WIDE // FINE) + k)
        low, high = scal[at], scal[at + 1]
        base = jnp.minimum(low // LANES * LANES, rows - WINDOW)
        cells.append((slice(k * FINE, (k + 1) * FINE), base, high))

    def one(lanes, base, w):
        low = base + w * WINDOW
        first = pl.multiple_of(jnp.minimum(low, rows - WINDOW), LANES)
        idx = idx_ref[:, lanes]
        idx = jnp.where(idx >= low, idx - first, -1)
        visit(lanes, pl.ds(first, WINDOW), one_hot(idx, 0, WINDOW))

    for lanes, base, _ in cells:
        one(lanes, base, 0)
    for lanes, base, high in cells:

        @pl.when(high >= base + WINDOW)
        def _():
            turns = (high - base) // WINDOW + 1
            lax.fori_loop(1, turns, lambda w, _: one(lanes, base, w), None)


def gather_kernel(scal, idx_ref, table_ref, out_ref, acc):
    @pl.when(live(scal, WIDE))
    def _():
        acc[...] = jnp.zeros_like(acc)

        def visit(lanes, rows, hot):
            acc[:, lanes] += mm(table_ref[:, rows], hot)

        over_windows(scal, table_ref.shape[1], idx_ref, visit)
        out_ref[...] = acc[...].astype(out_ref.dtype)


def negatives_kernel(scal, idx_ref, table_ref, out_ref):
    rows, chunk = table_ref.shape[1], 1024
    pieces = [(b, table_ref[:, b : b + chunk]) for b in range(0, rows, chunk)]
    out_ref[...] = table_rows(idx_ref[...], pieces).astype(out_ref.dtype)


def relation_gather_kernel(scal, idx_ref, table_ref, out_ref):
    @pl.when(live(scal))
    def _():
        both = table_rows(idx_ref[...], [(0, table_ref[...])])
        half = both.shape[0] // 2
        out_ref[...] = both[:half] + both[half:]


def valid_lanes(scal):
    lane = lax.broadcasted_iota(I32, (1, BLOCK), 1) + pl.program_id(0) * BLOCK
    return jnp.where(lane < scal[0], 1.0, 0.0)


def negative_scores_kernel(scal, s_ref, r_ref, neg_t_ref, half_neg_ref, gu_ref, gn_ref, acc):
    i = pl.program_id(0)

    @pl.when(i == 0)
    def _():
        acc[...] = jnp.zeros_like(acc)

    @pl.when(live(scal))
    def _():
        ub = (s_ref[...].astype(F32) * r_ref[...]).astype(BF16)
        half = mm(half_neg_ref[...], ub)
        weight = valid_lanes(scal) * (0.5 / half.shape[0])
        gneg = (jnp.tanh(half) * weight + weight).astype(BF16)
        gu_ref[...] = mm(neg_t_ref[...], gneg)
        acc[...] += mm_nt(ub, gneg)

    @pl.when(i == pl.num_programs(0) - 1)
    def _():
        gn_ref[...] = acc[...].astype(BF16)


def target_kernel(order, rows, scal, s_ref, r_ref, gun_ref, idx_ref, *refs):
    gn_ref, n_idx_ref, tables = refs[0], refs[1], refs[2 : 2 + len(order)]
    gs_ref, gr_ref, keep_ref, send_ref, t_acc, gt_scr, acc = refs[2 + len(order) :]
    i = pl.program_id(0)
    parts = 2 * acc.shape[0]
    sums = [(keep_ref, acc)[apart % 2].at[apart // 2] for apart in range(parts)]
    bases = [(scal[1] ^ apart) * rows for apart in range(parts)]

    @pl.when(i == 0)
    def _():
        for total, base in zip(sums, bases, strict=True):
            total[...] = mm_nt(gn_ref[...], one_hot(n_idx_ref[...], base, rows))

    @pl.when(live(scal))
    def _():
        spanned = span(scal, 2, BLOCK)
        t_acc[...] = jnp.zeros_like(t_acc)
        for apart, base in enumerate(bases):

            @pl.when(meets(spanned, base, rows))
            def _():
                pieces = [
                    (base + first, table[...])
                    for (k, first), table in zip(order, tables, strict=True)
                    if k == apart
                ]
                t_acc[...] += table_rows(idx_ref[...], pieces)

        t = t_acc[...]
        s = s_ref[...].astype(F32)
        r = r_ref[...]
        u = s * r
        pos = jnp.sum(u * t, axis=0, keepdims=True)
        gpos = -jax.nn.sigmoid(-pos) * valid_lanes(scal)
        gu = gpos * t + gun_ref[...]
        gs_ref[...] = (gu * r).astype(BF16)
        gr_ref[...] = (gu * s).astype(BF16)
        gt_scr[...] = (gpos * u).astype(BF16)
        for total, base in zip(sums, bases, strict=True):

            @pl.when(meets(spanned, base, rows))
            def _():
                total[...] += mm_nt(gt_scr[...], one_hot(idx_ref[...], base, rows))

    @pl.when(jnp.logical_not(live(scal)))
    def _():
        gs_ref[...] = jnp.zeros_like(gs_ref)
        gr_ref[...] = jnp.zeros_like(gr_ref)

    @pl.when(i == pl.num_programs(0) - 1)
    def _():
        send_ref[...] = acc[...].astype(BF16)


def relation_scatter_kernel(scal, g_ref, idx_ref, keep_ref, send_ref, acc):
    i = pl.program_id(0)

    @pl.when(i == 0)
    def _():
        acc[...] = jnp.zeros_like(acc)

    @pl.when(live(scal, WIDE))
    def _():
        acc[...] += mm_nt(g_ref[...], one_hot(idx_ref[...], 0, acc.shape[1]))

    def copy(core):
        for part, cell, slot, rows, cols in tiles((2, *keep_ref.shape), acc.shape):
            to = (keep_ref, send_ref)[part ^ core]
            at = (cell ^ (scal[2] & 15), pl.ds(slot * SUBLANES, SUBLANES))
            if rows is None:
                to[at] = jnp.zeros((SUBLANES, LANES), F32)
            else:
                to[at] = acc[rows, cols]

    for core in range(2):

        @pl.when((i == pl.num_programs(0) - 1) & (scal[1] & 1 == core))
        def _():
            copy(core)


def tiles(packed, flat):
    parts, cells, rows, _ = packed
    slots = rows // SUBLANES
    wide = flat[1] // parts // LANES
    for part in range(parts):
        for tile in range(cells * slots):
            cell, slot = divmod(tile, slots)
            row, col = divmod(tile, wide)
            if row * SUBLANES >= flat[0]:
                yield part, cell, slot, None, None
            else:
                row, col = row * SUBLANES, (part * wide + col) * LANES
                yield part, cell, slot, slice(row, row + SUBLANES), slice(col, col + LANES)


def scatter_kernel(scal, g_ref, idx_ref, keep_ref, send_ref, acc):
    i = pl.program_id(0)

    @pl.when(i == 0)
    def _():
        acc[...] = jnp.zeros_like(acc)

    @pl.when(live(scal, WIDE))
    def _():
        def visit(lanes, rows, hot):
            acc[:, rows] += mm_nt(g_ref[:, lanes], hot)

        over_windows(scal, acc.shape[1], idx_ref, visit)

    @pl.when(i == pl.num_programs(0) - 1)
    def _():
        rows = keep_ref.shape[2]
        for apart in range(acc.shape[1] // rows):
            part = acc[:, pl.ds(pl.multiple_of((scal[1] ^ apart) * rows, rows), rows)]
            to = (keep_ref, send_ref)[apart % 2]
            to[apart // 2] = part.astype(to.dtype)


def relation_update_kernel(scal, rel_ref, state_ref, near_ref, core_ref, *refs):
    new_rel_ref, new_state_ref, flat = refs
    parts, cells, rows, _ = flat.shape
    for k, g_ref in enumerate((near_ref, core_ref)):
        for cell in range(cells):
            away = cell ^ (scal[2] & 15)
            flat[(scal[1] & 1) ^ k, cell] = g_ref[away & 3, away >> 2].astype(F32)
    width, count = rel_ref.shape
    wide = -(-count // (parts * LANES)) * parts * LANES
    pieces = {}
    for part, cell, slot, trows, tcols in tiles(flat.shape, (width, wide)):
        if trows is not None:
            pieces[trows.start, tcols.start] = (part, cell, pl.ds(slot * SUBLANES, SUBLANES))
    for col in range(0, count, LANES):
        n = min(LANES, count - col)
        square = jnp.zeros((SUBLANES, LANES), F32)
        for row in range(0, width, SUBLANES):
            g = flat[pieces[row, col]]
            square = square + g * g
        mean = jnp.sum(square, axis=0, keepdims=True) * (1.0 / width)
        state = state_ref[:, col : col + n] + mean[:, :n]
        new_state_ref[:, col : col + n] = state
        scale = RATE / jnp.sqrt(state)
        for row in range(0, width, SUBLANES):
            at = (slice(row, row + SUBLANES), slice(col, col + n))
            new_rel_ref[at] = rel_ref[at] - flat[pieces[row, col]][:, :n] * scale


def after(x, *others):
    return lax.optimization_barrier((x, *others))[0]


def summed(x, axis, step):
    got = [swapped(x[k], axis, k * step).astype(F32) for k in (1, 2, 3)]
    return (x[0] + got[0]) + (got[1] + got[2])


def collected(x, axis, step):
    return jnp.stack([x] + [swapped(x, axis, k * step) for k in (1, 2, 3)])


def body(
    entity_slab,
    entity_state,
    relation_diag,
    relation_state,
    edge_source,
    edge_target,
    edge_relation,
    edge_count,
    negatives,
):
    slab = entity_slab.T
    relations = relation_diag.T
    width, rows_part = slab.shape
    reps = lax.axis_size("rep")
    half = lax.axis_size("dom") // 2
    quarter = rows_part // reps
    rep, dom = lax.axis_index("rep"), lax.axis_index("dom")
    edges, n_neg, n_rel = edge_source.shape[0], negatives.shape[0], relation_diag.shape[0]
    f32_of = lambda *shape: jax.ShapeDtypeStruct(shape, F32)
    bf16_of = lambda *shape: jax.ShapeDtypeStruct(shape, BF16)

    asked = swapped(negatives, "dom", half).reshape(1, n_neg)
    own = lax.dynamic_slice_in_dim(slab, rep * quarter, quarter, 1)
    step = quarter // PIECES
    own_pieces = [own[:, k * step : (k + 1) * step] for k in range(PIECES)]

    lane = jnp.arange(edges, dtype=I32)
    is_live = lane < edge_count[0]
    group = edge_target // quarter
    along = jnp.where(group % 2 == 0, edge_source, rows_part - 1 - edge_source)
    key = jnp.where(is_live, group * rows_part + along, reps * rows_part)
    _, src, dst, rel = lax.sort((key, edge_source, edge_target, edge_relation), num_keys=1)
    spans = []
    for idx in (src, dst):
        by_cell = idx.reshape(-1, FINE)
        cell_live = is_live.reshape(-1, FINE)
        spans.append(jnp.min(jnp.where(cell_live, by_cell, rows_part), axis=1))
        spans.append(jnp.max(jnp.where(cell_live, by_cell, -1), axis=1))
    fixed = jnp.stack([edge_count[0], rep.astype(I32), dom.astype(I32)])
    scal = jnp.concatenate([fixed, jnp.stack(spans, axis=1).reshape(-1)])
    src, dst, rel = (x.reshape(1, edges) for x in (src, dst, rel))

    quarter_neg = n_neg // reps
    found = call(
        negatives_kernel,
        "partner_negatives",
        1,
        [whole((1, quarter_neg)), whole(slab.shape)],
        whole((width, quarter_neg)),
        bf16_of(width, quarter_neg),
        [],
        fixed,
        lax.dynamic_slice_in_dim(asked, rep * quarter_neg, quarter_neg, 1),
        slab,
    )
    neg_far = swapped_far(found, half, 2)
    own_pieces[1:] = [after(x, found) for x in own_pieces[1:]]
    far = [swapped_far(x, half, 2) for x in own_pieces]
    s_rows = call(
        gather_kernel,
        "source_rows",
        edges // WIDE,
        [edge_block(1, WIDE), whole(slab.shape)],
        edge_block(width, WIDE),
        bf16_of(width, edges),
        [pltpu.VMEM((width, WIDE), F32)],
        scal,
        after(src, found),
        slab,
    )
    wide = -(-n_rel // (2 * LANES)) * 2 * LANES
    padded = jnp.pad(relations, ((0, 0), (0, wide - n_rel)))
    high = padded.astype(BF16)
    low = (padded - high.astype(F32)).astype(BF16)
    split = jnp.concatenate([high, low], axis=0)
    split = after(split, s_rows)
    r_rows = call(
        relation_gather_kernel,
        "relation_rows",
        edges // BLOCK,
        [edge_block(1), whole(split.shape)],
        edge_block(width),
        f32_of(width, edges),
        [],
        scal,
        rel,
        split,
    )
    neg_far = after(neg_far, split)
    neg_near = swapped(neg_far, "rep", 2)
    neg_far_core = swapped(neg_far, "rep", 1)
    neg_near = after(neg_near, r_rows)
    neg_near_core = swapped(neg_near, "rep", 1)
    neg_t = jnp.concatenate([neg_far, neg_near, neg_far_core, neg_near_core], axis=1)
    apart_by = (2, 0, 3, 1)
    neg_idx = jnp.concatenate(
        [
            lax.dynamic_slice_in_dim(negatives, (rep ^ k) * quarter_neg, quarter_neg, 0)
            for k in apart_by
        ]
    ).reshape(1, n_neg)
    half_neg = 0.5 * neg_t.T
    far = [after(x, r_rows) for x in far]
    near = [swapped(x, "rep", 2) for x in far]
    far_core = [swapped(x, "rep", 1) for x in far]
    gu_neg, grad_n = call(
        negative_scores_kernel,
        "negative_scores",
        edges // BLOCK,
        [edge_block(width), edge_block(width), whole((width, n_neg)), whole((n_neg, width))],
        [edge_block(width), whole((width, n_neg))],
        [f32_of(width, edges), bf16_of(width, n_neg)],
        [pltpu.VMEM((width, n_neg), F32)],
        scal,
        s_rows,
        r_rows,
        after(neg_t, *far),
        half_neg,
    )
    near = [after(x, gu_neg) for x in near]
    near_core = [swapped(x, "rep", 1) for x in near]
    tables = [*far, *near, *far_core, *near_core]
    order = tuple((k, piece * step) for k in apart_by for piece in range(PIECES))

    cells = 16
    slots = -(-(width // SUBLANES * wide // 2 // LANES) // cells)
    packed = (2, cells, slots * SUBLANES, LANES)
    half_parts = (reps // 2, width, quarter)
    grad_s, grad_r, dst_keep, dst_send = call(
        functools.partial(target_kernel, order, quarter),
        "targets",
        edges // BLOCK,
        [edge_block(width)] * 3
        + [edge_block(1)]
        + [whole((width, n_neg)), whole((1, n_neg))]
        + [whole(t.shape) for t in tables],
        [edge_block(width)] * 2 + [whole(half_parts)] * 2,
        [bf16_of(width, edges)] * 2 + [f32_of(*half_parts), bf16_of(*half_parts)],
        [
            pltpu.VMEM((width, BLOCK), F32),
            pltpu.VMEM((width, BLOCK), BF16),
            pltpu.VMEM(half_parts, F32),
        ],
        scal,
        s_rows,
        r_rows,
        gu_neg,
        dst,
        grad_n,
        neg_idx,
        *tables,
    )
    dst_sum = dst_keep + swapped(dst_send, "rep", 1).astype(F32)
    rel_keep, rel_send = call(
        relation_scatter_kernel,
        "relation_grads",
        edges // WIDE,
        [edge_block(width, WIDE), edge_block(1, WIDE)],
        [whole(packed[1:])] * 2,
        [f32_of(*packed[1:])] * 2,
        [pltpu.VMEM((width, wide), F32)],
        scal,
        after(grad_r, dst_sum),
        rel,
    )
    sent = [
        swapped(dst_sum[0, :, k * step : (k + 1) * step].astype(BF16), "rep", 2)
        for k in range(PIECES)
    ]
    sent = jnp.concatenate([after(x, rel_keep) for x in sent], axis=1)
    mine = (dst_sum[1] + sent.astype(F32)).astype(BF16)
    small = quarter // RETURNS
    returned = [
        swapped_far(mine[:, k * small : (k + 1) * small], half, 2) for k in range(RETURNS)
    ]
    src_keep, src_send = call(
        scatter_kernel,
        "source_grads",
        edges // WIDE,
        [edge_block(width, WIDE), edge_block(1, WIDE)],
        [whole(half_parts)] * 2,
        [f32_of(*half_parts), bf16_of(*half_parts)],
        [pltpu.VMEM((width, rows_part), F32)],
        scal,
        after(grad_s, mine),
        src,
    )

    grid = rel_keep + after(swapped(rel_send, "rep", 1), src_keep, *returned[: RETURNS // 2])
    grid = grid.reshape(4, 4, *packed[2:]).swapaxes(0, 1)
    line = summed([grid[0], *(grid[k].astype(BF16) for k in (1, 2, 3))], "dom", 1)
    cell = summed(line, "dom", 4)
    cell = after(cell, *returned[RETURNS // 2 :])
    cell = cell + swapped(cell, "rep", 2)
    total = summed([cell] * 4, "dom", 16).astype(BF16)
    src_sum = src_keep + swapped(src_send, "rep", 1).astype(F32)
    src_got = swapped(after(src_sum[1], total).astype(BF16), "rep", 2)
    line = collected(total, "dom", 4)
    grid = after(collected(line, "dom", 1), src_got)
    grid_core = swapped(grid, "rep", 1)

    kept = src_sum[0] + src_got.astype(F32)
    grads = kept + jnp.concatenate(returned, axis=1).astype(F32)

    new_state = entity_state + jnp.mean(grads * grads, axis=0)
    new_slab = (own.astype(F32) - RATE * grads / jnp.sqrt(new_state)[None, :]).astype(BF16)
    new_relation, new_relation_state = call(
        relation_update_kernel,
        "relation_update",
        1,
        [whole((width, n_rel)), whole((1, n_rel))] + [whole(grid.shape)] * 2,
        [whole((width, n_rel)), whole((1, n_rel))],
        [f32_of(width, n_rel), f32_of(1, n_rel)],
        [pltpu.VMEM(packed, F32)],
        fixed,
        relations,
        relation_state.reshape(1, n_rel),
        grid,
        grid_core,
    )
    return (new_slab.T, new_state, new_relation.T, new_relation_state.reshape(n_rel))


def solution(mesh):
    in_specs = (
        P("dom", None),
        P(("dom", "rep")),
        P(),
        P(),
        P(("dom", "rep")),
        P(("dom", "rep")),
        P(("dom", "rep")),
        P(("dom", "rep")),
        P("dom"),
    )
    out_specs = (P(("dom", "rep"), None), P(("dom", "rep")), P(), P())
    return jax.shard_map(body, mesh=mesh, in_specs=in_specs, out_specs=out_specs, check_vma=False)
```

```python
import functools

import jax
import jax.numpy as jnp
from jax import lax
from jax.experimental import pallas as pl
from jax.experimental.pallas import tpu as pltpu
from jax.sharding import PartitionSpec as P

BLOCK = 512
FINE = 256
WIDE = 1024
WINDOW = 1280
LANES = 128
SUBLANES = 8
PIECES = 2
VMEM_BYTES = 56 << 20
RATE = 0.1
BF16, F32, I32 = jnp.bfloat16, jnp.float32, jnp.int32


def swapped(x, axis, mask):
    return lax.ppermute(x, axis, [(i, i ^ mask) for i in range(lax.axis_size(axis))])


def swapped_far(x, dom_mask, rep_mask):
    doms, reps = lax.axis_size("dom"), lax.axis_size("rep")
    pairs = [
        (d * reps + r, (d ^ dom_mask) * reps + (r ^ rep_mask))
        for d in range(doms)
        for r in range(reps)
    ]
    return lax.ppermute(x, ("dom", "rep"), pairs)


def one_hot(idx, base, rows):
    row = lax.broadcasted_iota(I32, (rows, idx.shape[1]), 0)
    return jnp.where(row == idx - base, 1.0, 0.0).astype(BF16)


def mm(a, b):
    return jnp.dot(a, b, preferred_element_type=F32)


def mm_nt(a, b):
    return lax.dot_general(a, b, (((1,), (1,)), ((), ())), preferred_element_type=F32)


def call(kernel, name, grid, in_specs, out_specs, out_shape, scratch, *args, flops=0):
    return pl.pallas_call(
        kernel,
        grid_spec=pltpu.PrefetchScalarGridSpec(
            num_scalar_prefetch=1,
            grid=(grid,),
            in_specs=in_specs,
            out_specs=out_specs,
            scratch_shapes=scratch,
        ),
        out_shape=out_shape,
        compiler_params=pltpu.CompilerParams(vmem_limit_bytes=VMEM_BYTES),
        cost_estimate=pl.CostEstimate(flops=flops, bytes_accessed=0, transcendentals=0),
        name=name,
    )(*args)


def whole(shape):
    return pl.BlockSpec(shape, lambda i, c: (0,) * len(shape))


def edge_block(rows, block=BLOCK):
    return pl.BlockSpec((rows, block), lambda i, c: (0, i))


def live(scal, block=BLOCK):
    return pl.program_id(0) * block < scal[0]


def span(scal, which, block):
    each = block // FINE
    at = 3 + which
    first, last = None, None
    for k in range(each):
        cell = at + 4 * (pl.program_id(0) * each + k)
        low, high = scal[cell], scal[cell + 1]
        first = low if first is None else jnp.minimum(first, low)
        last = high if last is None else jnp.maximum(last, high)
    return first, last


def meets(spanned, base, rows):
    return (spanned[0] < base + rows) & (spanned[1] >= base)


def table_rows(idx, pieces):
    total = None
    for base, piece in pieces:
        y = mm(piece, one_hot(idx, base, piece.shape[1]))
        total = y if total is None else total + y
    return total


def over_windows(scal, rows, idx_ref, visit):
    cells = []
    for k in range(WIDE // FINE):
        at = 3 + 4 * (pl.program_id(0) * (WIDE // FINE) + k)
        low, high = scal[at], scal[at + 1]
        base = jnp.minimum(low // LANES * LANES, rows - WINDOW)
        cells.append((slice(k * FINE, (k + 1) * FINE), base, high))

    def one(lanes, base, w):
        low = base + w * WINDOW
        first = pl.multiple_of(jnp.minimum(low, rows - WINDOW), LANES)
        idx = idx_ref[:, lanes]
        idx = jnp.where(idx >= low, idx - first, -1)
        visit(lanes, pl.ds(first, WINDOW), one_hot(idx, 0, WINDOW))

    for lanes, base, _ in cells:
        one(lanes, base, 0)
    for lanes, base, high in cells:

        @pl.when(high >= base + WINDOW)
        def _():
            turns = (high - base) // WINDOW + 1
            lax.fori_loop(1, turns, lambda w, _: one(lanes, base, w), None)


def gather_kernel(scal, idx_ref, table_ref, out_ref, acc):
    @pl.when(live(scal, WIDE))
    def _():
        acc[...] = jnp.zeros_like(acc)

        def visit(lanes, rows, hot):
            acc[:, lanes] += mm(table_ref[:, rows], hot)

        over_windows(scal, table_ref.shape[1], idx_ref, visit)
        out_ref[...] = acc[...].astype(out_ref.dtype)


def negatives_kernel(scal, idx_ref, table_ref, out_ref):
    rows, chunk = table_ref.shape[1], 1024
    pieces = [(b, table_ref[:, b : b + chunk]) for b in range(0, rows, chunk)]
    out_ref[...] = table_rows(idx_ref[...], pieces).astype(out_ref.dtype)


def relation_gather_kernel(scal, idx_ref, table_ref, out_ref):
    @pl.when(live(scal))
    def _():
        both = table_rows(idx_ref[...], [(0, table_ref[...])])
        half = both.shape[0] // 2
        out_ref[...] = both[:half] + both[half:]


def valid_lanes(scal):
    lane = lax.broadcasted_iota(I32, (1, BLOCK), 1) + pl.program_id(0) * BLOCK
    return jnp.where(lane < scal[0], 1.0, 0.0)


def negative_scores_kernel(scal, s_ref, r_ref, neg_t_ref, half_neg_ref, gu_ref, gn_ref, acc):
    i = pl.program_id(0)

    @pl.when(i == 0)
    def _():
        acc[...] = jnp.zeros_like(acc)

    @pl.when(live(scal))
    def _():
        ub = (s_ref[...].astype(F32) * r_ref[...]).astype(BF16)
        half = mm(half_neg_ref[...], ub)
        weight = valid_lanes(scal) * (0.5 / half.shape[0])
        gneg = (jnp.tanh(half) * weight + weight).astype(BF16)
        gu_ref[...] = mm(neg_t_ref[...], gneg)
        acc[...] += mm_nt(ub, gneg)

    @pl.when(i == pl.num_programs(0) - 1)
    def _():
        gn_ref[...] = acc[...].astype(BF16)


def target_kernel(order, rows, scal, s_ref, r_ref, gun_ref, idx_ref, *refs):
    gn_ref, n_idx_ref, tables = refs[0], refs[1], refs[2 : 2 + len(order)]
    gs_ref, gr_ref, keep_ref, send_ref, t_acc, gt_scr, acc = refs[2 + len(order) :]
    i = pl.program_id(0)
    parts = 2 * acc.shape[0]
    sums = [(keep_ref, acc)[apart % 2].at[apart // 2] for apart in range(parts)]
    bases = [(scal[1] ^ apart) * rows for apart in range(parts)]

    @pl.when(i == 0)
    def _():
        for total, base in zip(sums, bases, strict=True):
            total[...] = mm_nt(gn_ref[...], one_hot(n_idx_ref[...], base, rows))

    @pl.when(live(scal))
    def _():
        spanned = span(scal, 2, BLOCK)
        t_acc[...] = jnp.zeros_like(t_acc)
        for apart, base in enumerate(bases):

            @pl.when(meets(spanned, base, rows))
            def _():
                pieces = [
                    (base + first, table[...])
                    for (k, first), table in zip(order, tables, strict=True)
                    if k == apart
                ]
                t_acc[...] += table_rows(idx_ref[...], pieces)

        t = t_acc[...]
        s = s_ref[...].astype(F32)
        r = r_ref[...]
        u = s * r
        pos = jnp.sum(u * t, axis=0, keepdims=True)
        gpos = -jax.nn.sigmoid(-pos) * valid_lanes(scal)
        gu = gpos * t + gun_ref[...]
        gs_ref[...] = (gu * r).astype(BF16)
        gr_ref[...] = (gu * s).astype(BF16)
        gt_scr[...] = (gpos * u).astype(BF16)
        for total, base in zip(sums, bases, strict=True):

            @pl.when(meets(spanned, base, rows))
            def _():
                total[...] += mm_nt(gt_scr[...], one_hot(idx_ref[...], base, rows))

    @pl.when(jnp.logical_not(live(scal)))
    def _():
        gs_ref[...] = jnp.zeros_like(gs_ref)
        gr_ref[...] = jnp.zeros_like(gr_ref)

    @pl.when(i == pl.num_programs(0) - 1)
    def _():
        send_ref[...] = acc[...].astype(BF16)


def relation_scatter_kernel(scal, g_ref, idx_ref, keep_ref, send_ref, acc):
    i = pl.program_id(0)

    @pl.when(i == 0)
    def _():
        acc[...] = jnp.zeros_like(acc)

    @pl.when(live(scal, WIDE))
    def _():
        acc[...] += mm_nt(g_ref[...], one_hot(idx_ref[...], 0, acc.shape[1]))

    def copy(core):
        for part, cell, slot, rows, cols in tiles((2, *keep_ref.shape), acc.shape):
            to = (keep_ref, send_ref)[part ^ core]
            at = (cell ^ (scal[2] & 15), pl.ds(slot * SUBLANES, SUBLANES))
            if rows is None:
                to[at] = jnp.zeros((SUBLANES, LANES), F32)
            else:
                to[at] = acc[rows, cols]

    for core in range(2):

        @pl.when((i == pl.num_programs(0) - 1) & (scal[1] & 1 == core))
        def _():
            copy(core)


def tiles(packed, flat):
    parts, cells, rows, _ = packed
    slots = rows // SUBLANES
    wide = flat[1] // parts // LANES
    for part in range(parts):
        for tile in range(cells * slots):
            cell, slot = divmod(tile, slots)
            row, col = divmod(tile, wide)
            if row * SUBLANES >= flat[0]:
                yield part, cell, slot, None, None
            else:
                row, col = row * SUBLANES, (part * wide + col) * LANES
                yield part, cell, slot, slice(row, row + SUBLANES), slice(col, col + LANES)


def scatter_kernel(scal, g_ref, idx_ref, keep_ref, send_ref, acc):
    i = pl.program_id(0)

    @pl.when(i == 0)
    def _():
        acc[...] = jnp.zeros_like(acc)

    @pl.when(live(scal, WIDE))
    def _():
        def visit(lanes, rows, hot):
            acc[:, rows] += mm_nt(g_ref[:, lanes], hot)

        over_windows(scal, acc.shape[1], idx_ref, visit)

    @pl.when(i == pl.num_programs(0) - 1)
    def _():
        rows = keep_ref.shape[2]
        for apart in range(acc.shape[1] // rows):
            part = acc[:, pl.ds(pl.multiple_of((scal[1] ^ apart) * rows, rows), rows)]
            to = (keep_ref, send_ref)[apart % 2]
            to[apart // 2] = part.astype(to.dtype)


def relation_update_kernel(scal, rel_ref, state_ref, near_ref, core_ref, *refs):
    new_rel_ref, new_state_ref, flat = refs
    parts, cells, rows, _ = flat.shape
    for k, g_ref in enumerate((near_ref, core_ref)):
        for cell in range(cells):
            away = cell ^ (scal[2] & 15)
            flat[(scal[1] & 1) ^ k, cell] = g_ref[away & 3, away >> 2].astype(F32)
    width, count = rel_ref.shape
    wide = -(-count // (parts * LANES)) * parts * LANES
    pieces = {}
    for part, cell, slot, trows, tcols in tiles(flat.shape, (width, wide)):
        if trows is not None:
            pieces[trows.start, tcols.start] = (part, cell, pl.ds(slot * SUBLANES, SUBLANES))
    for col in range(0, count, LANES):
        n = min(LANES, count - col)
        square = jnp.zeros((SUBLANES, LANES), F32)
        for row in range(0, width, SUBLANES):
            g = flat[pieces[row, col]]
            square = square + g * g
        mean = jnp.sum(square, axis=0, keepdims=True) * (1.0 / width)
        state = state_ref[:, col : col + n] + mean[:, :n]
        new_state_ref[:, col : col + n] = state
        scale = RATE / jnp.sqrt(state)
        for row in range(0, width, SUBLANES):
            at = (slice(row, row + SUBLANES), slice(col, col + n))
            new_rel_ref[at] = rel_ref[at] - flat[pieces[row, col]][:, :n] * scale


def after(x, *others):
    return lax.optimization_barrier((x, *others))[0]


def summed(x, axis, step):
    got = [swapped(x[k], axis, k * step).astype(F32) for k in (1, 2, 3)]
    return (x[0] + got[0]) + (got[1] + got[2])


def collected(x, axis, step):
    return jnp.stack([x] + [swapped(x, axis, k * step) for k in (1, 2, 3)])


def body(
    entity_slab,
    entity_state,
    relation_diag,
    relation_state,
    edge_source,
    edge_target,
    edge_relation,
    edge_count,
    negatives,
):
    slab = entity_slab.T
    relations = relation_diag.T
    width, rows_part = slab.shape
    reps = lax.axis_size("rep")
    half = lax.axis_size("dom") // 2
    quarter = rows_part // reps
    rep, dom = lax.axis_index("rep"), lax.axis_index("dom")
    edges, n_neg, n_rel = edge_source.shape[0], negatives.shape[0], relation_diag.shape[0]
    f32_of = lambda *shape: jax.ShapeDtypeStruct(shape, F32)
    bf16_of = lambda *shape: jax.ShapeDtypeStruct(shape, BF16)

    asked = swapped(negatives, "dom", half).reshape(1, n_neg)
    own = lax.dynamic_slice_in_dim(slab, rep * quarter, quarter, 1)
    step = quarter // PIECES
    own_pieces = [own[:, k * step : (k + 1) * step] for k in range(PIECES)]

    lane = jnp.arange(edges, dtype=I32)
    is_live = lane < edge_count[0]
    group = edge_target // quarter
    along = jnp.where(group % 2 == 0, edge_source, rows_part - 1 - edge_source)
    key = jnp.where(is_live, group * rows_part + along, reps * rows_part)
    _, src, dst, rel = lax.sort((key, edge_source, edge_target, edge_relation), num_keys=1)
    spans = []
    for idx in (src, dst):
        by_cell = idx.reshape(-1, FINE)
        cell_live = is_live.reshape(-1, FINE)
        spans.append(jnp.min(jnp.where(cell_live, by_cell, rows_part), axis=1))
        spans.append(jnp.max(jnp.where(cell_live, by_cell, -1), axis=1))
    fixed = jnp.stack([edge_count[0], rep.astype(I32), dom.astype(I32)])
    scal = jnp.concatenate([fixed, jnp.stack(spans, axis=1).reshape(-1)])
    src, dst, rel = (x.reshape(1, edges) for x in (src, dst, rel))

    quarter_neg = n_neg // reps
    found = call(
        negatives_kernel,
        "partner_negatives",
        1,
        [whole((1, quarter_neg)), whole(slab.shape)],
        whole((width, quarter_neg)),
        bf16_of(width, quarter_neg),
        [],
        fixed,
        lax.dynamic_slice_in_dim(asked, rep * quarter_neg, quarter_neg, 1),
        slab,
    )
    neg_far = swapped_far(found, half, 2)
    own_pieces[1:] = [after(x, found) for x in own_pieces[1:]]
    far = [swapped_far(x, half, 2) for x in own_pieces]
    s_rows = call(
        gather_kernel,
        "source_rows",
        edges // WIDE,
        [edge_block(1, WIDE), whole(slab.shape)],
        edge_block(width, WIDE),
        bf16_of(width, edges),
        [pltpu.VMEM((width, WIDE), F32)],
        scal,
        after(src, found),
        slab,
    )
    wide = -(-n_rel // (2 * LANES)) * 2 * LANES
    padded = jnp.pad(relations, ((0, 0), (0, wide - n_rel)))
    high = padded.astype(BF16)
    low = (padded - high.astype(F32)).astype(BF16)
    split = jnp.concatenate([high, low], axis=0)
    split = after(split, s_rows)
    r_rows = call(
        relation_gather_kernel,
        "relation_rows",
        edges // BLOCK,
        [edge_block(1), whole(split.shape)],
        edge_block(width),
        f32_of(width, edges),
        [],
        scal,
        rel,
        split,
    )
    neg_far = after(neg_far, split)
    neg_near = swapped(neg_far, "rep", 2)
    neg_far_core = swapped(neg_far, "rep", 1)
    neg_near = after(neg_near, r_rows)
    neg_near_core = swapped(neg_near, "rep", 1)
    neg_t = jnp.concatenate([neg_far, neg_near, neg_far_core, neg_near_core], axis=1)
    apart_by = (2, 0, 3, 1)
    neg_idx = jnp.concatenate(
        [
            lax.dynamic_slice_in_dim(negatives, (rep ^ k) * quarter_neg, quarter_neg, 0)
            for k in apart_by
        ]
    ).reshape(1, n_neg)
    half_neg = 0.5 * neg_t.T
    far = [after(x, r_rows) for x in far]
    near = [swapped(x, "rep", 2) for x in far]
    far_core = [swapped(x, "rep", 1) for x in far]
    gu_neg, grad_n = call(
        negative_scores_kernel,
        "negative_scores",
        edges // BLOCK,
        [edge_block(width), edge_block(width), whole((width, n_neg)), whole((n_neg, width))],
        [edge_block(width), whole((width, n_neg))],
        [f32_of(width, edges), bf16_of(width, n_neg)],
        [pltpu.VMEM((width, n_neg), F32)],
        scal,
        s_rows,
        r_rows,
        after(neg_t, *far),
        half_neg,
    )
    near = [after(x, gu_neg) for x in near]
    near_core = [swapped(x, "rep", 1) for x in near]
    tables = [*far, *near, *far_core, *near_core]
    order = tuple((k, piece * step) for k in apart_by for piece in range(PIECES))

    cells = 16
    slots = -(-(width // SUBLANES * wide // 2 // LANES) // cells)
    packed = (2, cells, slots * SUBLANES, LANES)
    half_parts = (reps // 2, width, quarter)
    grad_s, grad_r, dst_keep, dst_send = call(
        functools.partial(target_kernel, order, quarter),
        "targets",
        edges // BLOCK,
        [edge_block(width)] * 3
        + [edge_block(1)]
        + [whole((width, n_neg)), whole((1, n_neg))]
        + [whole(t.shape) for t in tables],
        [edge_block(width)] * 2 + [whole(half_parts)] * 2,
        [bf16_of(width, edges)] * 2 + [f32_of(*half_parts), bf16_of(*half_parts)],
        [
            pltpu.VMEM((width, BLOCK), F32),
            pltpu.VMEM((width, BLOCK), BF16),
            pltpu.VMEM(half_parts, F32),
        ],
        scal,
        s_rows,
        r_rows,
        gu_neg,
        dst,
        grad_n,
        neg_idx,
        *tables,
    )
    dst_sum = dst_keep + swapped(dst_send, "rep", 1).astype(F32)
    rel_keep, rel_send = call(
        relation_scatter_kernel,
        "relation_grads",
        edges // WIDE,
        [edge_block(width, WIDE), edge_block(1, WIDE)],
        [whole(packed[1:])] * 2,
        [f32_of(*packed[1:])] * 2,
        [pltpu.VMEM((width, wide), F32)],
        scal,
        after(grad_r, dst_sum),
        rel,
        flops=2 * width * wide * edges,
    )
    sent = [
        swapped(dst_sum[0, :, k * step : (k + 1) * step].astype(BF16), "rep", 2)
        for k in range(PIECES)
    ]
    first = dst_sum[1, :, :step] + after(sent[0], rel_keep).astype(F32)
    first = first.astype(BF16)
    returned = [swapped_far(first, half, 2)]
    src_keep, src_send = call(
        scatter_kernel,
        "source_grads",
        edges // WIDE,
        [edge_block(width, WIDE), edge_block(1, WIDE)],
        [whole(half_parts)] * 2,
        [f32_of(*half_parts), bf16_of(*half_parts)],
        [pltpu.VMEM((width, rows_part), F32)],
        scal,
        after(grad_s, first),
        src,
        flops=width * rows_part * edges,
    )

    last = dst_sum[1, :, step:] + after(sent[1], src_keep).astype(F32)
    last = last.astype(BF16)
    returned.append(swapped_far(last, half, 2))

    grid = rel_keep + after(swapped(rel_send, "rep", 1), src_keep, returned[0], last)
    grid = grid.reshape(4, 4, *packed[2:]).swapaxes(0, 1)
    line = summed([grid[0], *(grid[k].astype(BF16) for k in (1, 2, 3))], "dom", 1)
    cell = summed(line, "dom", 4)
    cell = after(cell, *returned[1:])
    cell = cell + swapped(cell, "rep", 2)
    total = summed([cell] * 4, "dom", 16).astype(BF16)
    src_sum = src_keep + swapped(src_send, "rep", 1).astype(F32)
    src_got = swapped(after(src_sum[1], total).astype(BF16), "rep", 2)
    line = collected(total, "dom", 4)
    grid = after(collected(line, "dom", 1), src_got)
    grid_core = swapped(grid, "rep", 1)

    kept = src_sum[0] + src_got.astype(F32)
    grads = kept + jnp.concatenate(returned, axis=1).astype(F32)

    new_state = entity_state + jnp.mean(grads * grads, axis=0)
    new_slab = (own.astype(F32) - RATE * grads / jnp.sqrt(new_state)[None, :]).astype(BF16)
    new_relation, new_relation_state = call(
        relation_update_kernel,
        "relation_update",
        1,
        [whole((width, n_rel)), whole((1, n_rel))] + [whole(grid.shape)] * 2,
        [whole((width, n_rel)), whole((1, n_rel))],
        [f32_of(width, n_rel), f32_of(1, n_rel)],
        [pltpu.VMEM(packed, F32)],
        fixed,
        relations,
        relation_state.reshape(1, n_rel),
        grid,
        grid_core,
    )
    return (new_slab.T, new_state, new_relation.T, new_relation_state.reshape(n_rel))


def solution(mesh):
    in_specs = (
        P("dom", None),
        P(("dom", "rep")),
        P(),
        P(),
        P(("dom", "rep")),
        P(("dom", "rep")),
        P(("dom", "rep")),
        P(("dom", "rep")),
        P("dom"),
    )
    out_specs = (P(("dom", "rep"), None), P(("dom", "rep")), P(), P())
    return jax.shard_map(body, mesh=mesh, in_specs=in_specs, out_specs=out_specs, check_vma=False)
```

```python
import functools

import jax
import jax.numpy as jnp
from jax import lax
from jax.experimental import pallas as pl
from jax.experimental.pallas import tpu as pltpu
from jax.sharding import PartitionSpec as P

BLOCK = 512
FINE = 256
WIDE = 1024
WINDOW = 1280
LANES = 128
SUBLANES = 8
PIECES = 2
VMEM_BYTES = 56 << 20
RATE = 0.1
BF16, F32, I32 = jnp.bfloat16, jnp.float32, jnp.int32


def swapped(x, axis, mask):
    return lax.ppermute(x, axis, [(i, i ^ mask) for i in range(lax.axis_size(axis))])


def swapped_far(x, dom_mask, rep_mask):
    doms, reps = lax.axis_size("dom"), lax.axis_size("rep")
    pairs = [
        (d * reps + r, (d ^ dom_mask) * reps + (r ^ rep_mask))
        for d in range(doms)
        for r in range(reps)
    ]
    return lax.ppermute(x, ("dom", "rep"), pairs)


def one_hot(idx, base, rows):
    row = lax.broadcasted_iota(I32, (rows, idx.shape[1]), 0)
    return jnp.where(row == idx - base, 1.0, 0.0).astype(BF16)


def mm(a, b):
    return jnp.dot(a, b, preferred_element_type=F32)


def mm_nt(a, b):
    return lax.dot_general(a, b, (((1,), (1,)), ((), ())), preferred_element_type=F32)


def call(kernel, name, grid, in_specs, out_specs, out_shape, scratch, *args, flops=0):
    return pl.pallas_call(
        kernel,
        grid_spec=pltpu.PrefetchScalarGridSpec(
            num_scalar_prefetch=1,
            grid=(grid,),
            in_specs=in_specs,
            out_specs=out_specs,
            scratch_shapes=scratch,
        ),
        out_shape=out_shape,
        compiler_params=pltpu.CompilerParams(vmem_limit_bytes=VMEM_BYTES),
        cost_estimate=pl.CostEstimate(flops=flops, bytes_accessed=0, transcendentals=0),
        name=name,
    )(*args)


def whole(shape):
    return pl.BlockSpec(shape, lambda i, c: (0,) * len(shape))


def edge_block(rows, block=BLOCK):
    return pl.BlockSpec((rows, block), lambda i, c: (0, i))


def live(scal, block=BLOCK):
    return pl.program_id(0) * block < scal[0]


def span(scal, which, block):
    each = block // FINE
    at = 3 + which
    first, last = None, None
    for k in range(each):
        cell = at + 4 * (pl.program_id(0) * each + k)
        low, high = scal[cell], scal[cell + 1]
        first = low if first is None else jnp.minimum(first, low)
        last = high if last is None else jnp.maximum(last, high)
    return first, last


def meets(spanned, base, rows):
    return (spanned[0] < base + rows) & (spanned[1] >= base)


def table_rows(idx, pieces):
    total = None
    for base, piece in pieces:
        y = mm(piece, one_hot(idx, base, piece.shape[1]))
        total = y if total is None else total + y
    return total


def over_windows(scal, rows, idx_ref, visit):
    cells = []
    for k in range(WIDE // FINE):
        at = 3 + 4 * (pl.program_id(0) * (WIDE // FINE) + k)
        low, high = scal[at], scal[at + 1]
        base = jnp.minimum(low // LANES * LANES, rows - WINDOW)
        cells.append((slice(k * FINE, (k + 1) * FINE), base, high))

    def one(lanes, base, w):
        low = base + w * WINDOW
        first = pl.multiple_of(jnp.minimum(low, rows - WINDOW), LANES)
        idx = idx_ref[:, lanes]
        idx = jnp.where(idx >= low, idx - first, -1)
        visit(lanes, pl.ds(first, WINDOW), one_hot(idx, 0, WINDOW))

    for lanes, base, _ in cells:
        one(lanes, base, 0)
    for lanes, base, high in cells:

        @pl.when(high >= base + WINDOW)
        def _():
            turns = (high - base) // WINDOW + 1
            lax.fori_loop(1, turns, lambda w, _: one(lanes, base, w), None)


def gather_kernel(scal, idx_ref, table_ref, out_ref, acc):
    @pl.when(live(scal, WIDE))
    def _():
        acc[...] = jnp.zeros_like(acc)

        def visit(lanes, rows, hot):
            acc[:, lanes] += mm(table_ref[:, rows], hot)

        over_windows(scal, table_ref.shape[1], idx_ref, visit)
        out_ref[...] = acc[...].astype(out_ref.dtype)


def negatives_kernel(scal, idx_ref, table_ref, out_ref):
    rows, chunk = table_ref.shape[1], 1024
    pieces = [(b, table_ref[:, b : b + chunk]) for b in range(0, rows, chunk)]
    out_ref[...] = table_rows(idx_ref[...], pieces).astype(out_ref.dtype)


def relation_gather_kernel(scal, idx_ref, table_ref, out_ref):
    @pl.when(live(scal))
    def _():
        both = table_rows(idx_ref[...], [(0, table_ref[...])])
        half = both.shape[0] // 2
        out_ref[...] = both[:half] + both[half:]


def valid_lanes(scal):
    lane = lax.broadcasted_iota(I32, (1, BLOCK), 1) + pl.program_id(0) * BLOCK
    return jnp.where(lane < scal[0], 1.0, 0.0)


def negative_scores_kernel(scal, s_ref, r_ref, neg_t_ref, half_neg_ref, gu_ref, gn_ref, acc):
    i = pl.program_id(0)

    @pl.when(i == 0)
    def _():
        acc[...] = jnp.zeros_like(acc)

    @pl.when(live(scal))
    def _():
        ub = (s_ref[...].astype(F32) * r_ref[...]).astype(BF16)
        half = mm(half_neg_ref[...], ub)
        weight = valid_lanes(scal) * (0.5 / half.shape[0])
        gneg = (jnp.tanh(half) * weight + weight).astype(BF16)
        gu_ref[...] = mm(neg_t_ref[...], gneg)
        acc[...] += mm_nt(ub, gneg)

    @pl.when(i == pl.num_programs(0) - 1)
    def _():
        gn_ref[...] = acc[...].astype(BF16)


def target_kernel(order, rows, scal, s_ref, r_ref, gun_ref, idx_ref, *refs):
    gn_ref, n_idx_ref, tables = refs[0], refs[1], refs[2 : 2 + len(order)]
    gs_ref, gr_ref, *keep_refs = refs[2 + len(order) : 6 + len(order)]
    *send_refs, t_acc, gt_scr, acc = refs[6 + len(order) :]
    i = pl.program_id(0)
    parts = 2 * acc.shape[0]
    sums = [acc.at[k // 2] if k % 2 else keep_refs[k // 2] for k in range(parts)]
    bases = [(scal[1] ^ apart) * rows for apart in range(parts)]

    @pl.when(i == 0)
    def _():
        for total, base in zip(sums, bases, strict=True):
            total[...] = mm_nt(gn_ref[...], one_hot(n_idx_ref[...], base, rows))

    @pl.when(live(scal))
    def _():
        spanned = span(scal, 2, BLOCK)
        t_acc[...] = jnp.zeros_like(t_acc)
        for apart, base in enumerate(bases):

            @pl.when(meets(spanned, base, rows))
            def _():
                pieces = [
                    (base + first, table[...])
                    for (k, first), table in zip(order, tables, strict=True)
                    if k == apart
                ]
                t_acc[...] += table_rows(idx_ref[...], pieces)

        t = t_acc[...]
        s = s_ref[...].astype(F32)
        r = r_ref[...]
        u = s * r
        pos = jnp.sum(u * t, axis=0, keepdims=True)
        gpos = -jax.nn.sigmoid(-pos) * valid_lanes(scal)
        gu = gpos * t + gun_ref[...]
        gs_ref[...] = (gu * r).astype(BF16)
        gr_ref[...] = (gu * s).astype(BF16)
        gt_scr[...] = (gpos * u).astype(BF16)
        for total, base in zip(sums, bases, strict=True):

            @pl.when(meets(spanned, base, rows))
            def _():
                total[...] += mm_nt(gt_scr[...], one_hot(idx_ref[...], base, rows))

    @pl.when(jnp.logical_not(live(scal)))
    def _():
        gs_ref[...] = jnp.zeros_like(gs_ref)
        gr_ref[...] = jnp.zeros_like(gr_ref)

    @pl.when(i == pl.num_programs(0) - 1)
    def _():
        for k, send_ref in enumerate(send_refs):
            send_ref[...] = acc[k].astype(BF16)


def relation_scatter_kernel(scal, g_ref, idx_ref, keep_ref, send_ref, acc):
    i = pl.program_id(0)

    @pl.when(i == 0)
    def _():
        acc[...] = jnp.zeros_like(acc)

    @pl.when(live(scal, WIDE))
    def _():
        acc[...] += mm_nt(g_ref[...], one_hot(idx_ref[...], 0, acc.shape[1]))

    def copy(core):
        for part, cell, slot, rows, cols in tiles((2, *keep_ref.shape), acc.shape):
            to = (keep_ref, send_ref)[part ^ core]
            at = (cell ^ (scal[2] & 15), pl.ds(slot * SUBLANES, SUBLANES))
            if rows is None:
                to[at] = jnp.zeros((SUBLANES, LANES), F32)
            else:
                to[at] = acc[rows, cols]

    for core in range(2):

        @pl.when((i == pl.num_programs(0) - 1) & (scal[1] & 1 == core))
        def _():
            copy(core)


def tiles(packed, flat):
    parts, cells, rows, _ = packed
    slots = rows // SUBLANES
    wide = flat[1] // parts // LANES
    for part in range(parts):
        for tile in range(cells * slots):
            cell, slot = divmod(tile, slots)
            row, col = divmod(tile, wide)
            if row * SUBLANES >= flat[0]:
                yield part, cell, slot, None, None
            else:
                row, col = row * SUBLANES, (part * wide + col) * LANES
                yield part, cell, slot, slice(row, row + SUBLANES), slice(col, col + LANES)


def scatter_kernel(scal, g_ref, idx_ref, keep_ref, send_ref, acc):
    i = pl.program_id(0)

    @pl.when(i == 0)
    def _():
        acc[...] = jnp.zeros_like(acc)

    @pl.when(live(scal, WIDE))
    def _():
        def visit(lanes, rows, hot):
            acc[:, rows] += mm_nt(g_ref[:, lanes], hot)

        over_windows(scal, acc.shape[1], idx_ref, visit)

    @pl.when(i == pl.num_programs(0) - 1)
    def _():
        rows = keep_ref.shape[2]
        for apart in range(acc.shape[1] // rows):
            part = acc[:, pl.ds(pl.multiple_of((scal[1] ^ apart) * rows, rows), rows)]
            to = (keep_ref, send_ref)[apart % 2]
            to[apart // 2] = part.astype(to.dtype)


def relation_update_kernel(scal, rel_ref, state_ref, near_ref, core_ref, *refs):
    new_rel_ref, new_state_ref, flat = refs
    parts, cells, rows, _ = flat.shape
    for k, g_ref in enumerate((near_ref, core_ref)):
        for cell in range(cells):
            away = cell ^ (scal[2] & 15)
            flat[(scal[1] & 1) ^ k, cell] = g_ref[away & 3, away >> 2].astype(F32)
    width, count = rel_ref.shape
    wide = -(-count // (parts * LANES)) * parts * LANES
    pieces = {}
    for part, cell, slot, trows, tcols in tiles(flat.shape, (width, wide)):
        if trows is not None:
            pieces[trows.start, tcols.start] = (part, cell, pl.ds(slot * SUBLANES, SUBLANES))
    for col in range(0, count, LANES):
        n = min(LANES, count - col)
        square = jnp.zeros((SUBLANES, LANES), F32)
        for row in range(0, width, SUBLANES):
            g = flat[pieces[row, col]]
            square = square + g * g
        mean = jnp.sum(square, axis=0, keepdims=True) * (1.0 / width)
        state = state_ref[:, col : col + n] + mean[:, :n]
        new_state_ref[:, col : col + n] = state
        scale = RATE / jnp.sqrt(state)
        for row in range(0, width, SUBLANES):
            at = (slice(row, row + SUBLANES), slice(col, col + n))
            new_rel_ref[at] = rel_ref[at] - flat[pieces[row, col]][:, :n] * scale


def after(x, *others):
    return lax.optimization_barrier((x, *others))[0]


def summed(x, axis, step):
    got = [swapped(x[k], axis, k * step).astype(F32) for k in (1, 2, 3)]
    return (x[0] + got[0]) + (got[1] + got[2])


def collected(x, axis, step):
    return jnp.stack([x] + [swapped(x, axis, k * step) for k in (1, 2, 3)])


def body(
    entity_slab,
    entity_state,
    relation_diag,
    relation_state,
    edge_source,
    edge_target,
    edge_relation,
    edge_count,
    negatives,
):
    slab = entity_slab.T
    relations = relation_diag.T
    width, rows_part = slab.shape
    reps = lax.axis_size("rep")
    half = lax.axis_size("dom") // 2
    quarter = rows_part // reps
    rep, dom = lax.axis_index("rep"), lax.axis_index("dom")
    edges, n_neg, n_rel = edge_source.shape[0], negatives.shape[0], relation_diag.shape[0]
    f32_of = lambda *shape: jax.ShapeDtypeStruct(shape, F32)
    bf16_of = lambda *shape: jax.ShapeDtypeStruct(shape, BF16)

    asked = swapped(negatives, "dom", half).reshape(1, n_neg)
    own = lax.dynamic_slice_in_dim(slab, rep * quarter, quarter, 1)
    step = quarter // PIECES
    own_pieces = [own[:, k * step : (k + 1) * step] for k in range(PIECES)]

    lane = jnp.arange(edges, dtype=I32)
    is_live = lane < edge_count[0]
    group = edge_target // quarter
    along = jnp.where(group % 2 == 0, edge_source, rows_part - 1 - edge_source)
    key = jnp.where(is_live, group * rows_part + along, reps * rows_part)
    _, src, dst, rel = lax.sort((key, edge_source, edge_target, edge_relation), num_keys=1)
    spans = []
    for idx in (src, dst):
        by_cell = idx.reshape(-1, FINE)
        cell_live = is_live.reshape(-1, FINE)
        spans.append(jnp.min(jnp.where(cell_live, by_cell, rows_part), axis=1))
        spans.append(jnp.max(jnp.where(cell_live, by_cell, -1), axis=1))
    fixed = jnp.stack([edge_count[0], rep.astype(I32), dom.astype(I32)])
    scal = jnp.concatenate([fixed, jnp.stack(spans, axis=1).reshape(-1)])
    src, dst, rel = (x.reshape(1, edges) for x in (src, dst, rel))

    quarter_neg = n_neg // reps
    found = call(
        negatives_kernel,
        "partner_negatives",
        1,
        [whole((1, quarter_neg)), whole(slab.shape)],
        whole((width, quarter_neg)),
        bf16_of(width, quarter_neg),
        [],
        fixed,
        lax.dynamic_slice_in_dim(asked, rep * quarter_neg, quarter_neg, 1),
        slab,
    )
    neg_far = swapped_far(found, half, 2)
    own_pieces[1:] = [after(x, found) for x in own_pieces[1:]]
    far = [swapped_far(x, half, 2) for x in own_pieces]
    s_rows = call(
        gather_kernel,
        "source_rows",
        edges // WIDE,
        [edge_block(1, WIDE), whole(slab.shape)],
        edge_block(width, WIDE),
        bf16_of(width, edges),
        [pltpu.VMEM((width, WIDE), F32)],
        scal,
        after(src, found),
        slab,
    )
    wide = -(-n_rel // (2 * LANES)) * 2 * LANES
    padded = jnp.pad(relations, ((0, 0), (0, wide - n_rel)))
    high = padded.astype(BF16)
    low = (padded - high.astype(F32)).astype(BF16)
    split = jnp.concatenate([high, low], axis=0)
    split = after(split, s_rows)
    r_rows = call(
        relation_gather_kernel,
        "relation_rows",
        edges // BLOCK,
        [edge_block(1), whole(split.shape)],
        edge_block(width),
        f32_of(width, edges),
        [],
        scal,
        rel,
        split,
    )
    neg_far = after(neg_far, split)
    neg_near = swapped(neg_far, "rep", 2)
    neg_far_core = swapped(neg_far, "rep", 1)
    neg_near = after(neg_near, r_rows)
    neg_near_core = swapped(neg_near, "rep", 1)
    neg_t = jnp.concatenate([neg_far, neg_near, neg_far_core, neg_near_core], axis=1)
    apart_by = (2, 0, 3, 1)
    neg_idx = jnp.concatenate(
        [
            lax.dynamic_slice_in_dim(negatives, (rep ^ k) * quarter_neg, quarter_neg, 0)
            for k in apart_by
        ]
    ).reshape(1, n_neg)
    half_neg = 0.5 * neg_t.T
    far = [after(x, r_rows) for x in far]
    near = [swapped(x, "rep", 2) for x in far]
    far_core = [swapped(x, "rep", 1) for x in far]
    gu_neg, grad_n = call(
        negative_scores_kernel,
        "negative_scores",
        edges // BLOCK,
        [edge_block(width), edge_block(width), whole((width, n_neg)), whole((n_neg, width))],
        [edge_block(width), whole((width, n_neg))],
        [f32_of(width, edges), bf16_of(width, n_neg)],
        [pltpu.VMEM((width, n_neg), F32)],
        scal,
        s_rows,
        r_rows,
        after(neg_t, *far),
        half_neg,
    )
    near = [after(x, gu_neg) for x in near]
    near_core = [swapped(x, "rep", 1) for x in near]
    tables = [*far, *near, *far_core, *near_core]
    order = tuple((k, piece * step) for k in apart_by for piece in range(PIECES))

    cells = 16
    slots = -(-(width // SUBLANES * wide // 2 // LANES) // cells)
    packed = (2, cells, slots * SUBLANES, LANES)
    half_parts = (reps // 2, width, quarter)
    part = (width, quarter)
    grad_s, grad_r, keep_on, keep_back, send_on, send_back = call(
        functools.partial(target_kernel, order, quarter),
        "targets",
        edges // BLOCK,
        [edge_block(width)] * 3
        + [edge_block(1)]
        + [whole((width, n_neg)), whole((1, n_neg))]
        + [whole(t.shape) for t in tables],
        [edge_block(width)] * 2 + [whole(part)] * 4,
        [bf16_of(width, edges)] * 2 + [f32_of(*part)] * 2 + [bf16_of(*part)] * 2,
        [
            pltpu.VMEM((width, BLOCK), F32),
            pltpu.VMEM((width, BLOCK), BF16),
            pltpu.VMEM(half_parts, F32),
        ],
        scal,
        s_rows,
        r_rows,
        gu_neg,
        dst,
        grad_n,
        neg_idx,
        *tables,
    )
    on = (keep_on + swapped(send_on, "rep", 1).astype(F32)).astype(BF16)
    sent = [swapped(on[:, k * step : (k + 1) * step], "rep", 2) for k in range(PIECES)]
    rel_keep, rel_send = call(
        relation_scatter_kernel,
        "relation_grads",
        edges // WIDE,
        [edge_block(width, WIDE), edge_block(1, WIDE)],
        [whole(packed[1:])] * 2,
        [f32_of(*packed[1:])] * 2,
        [pltpu.VMEM((width, wide), F32)],
        scal,
        after(grad_r, on),
        rel,
        flops=2 * width * wide * edges,
    )
    back = keep_back + after(swapped(send_back, "rep", 1), rel_keep).astype(F32)
    first = back[:, :step] + after(sent[0], rel_keep).astype(F32)
    first = first.astype(BF16)
    returned = [swapped_far(first, half, 2)]
    src_keep, src_send = call(
        scatter_kernel,
        "source_grads",
        edges // WIDE,
        [edge_block(width, WIDE), edge_block(1, WIDE)],
        [whole(half_parts)] * 2,
        [f32_of(*half_parts), bf16_of(*half_parts)],
        [pltpu.VMEM((width, rows_part), F32)],
        scal,
        after(grad_s, first),
        src,
        flops=width * rows_part * edges,
    )

    last = back[:, step:] + after(sent[1], src_keep).astype(F32)
    last = last.astype(BF16)
    returned.append(swapped_far(last, half, 2))

    grid = rel_keep + after(swapped(rel_send, "rep", 1), src_keep, returned[0], last)
    grid = grid.reshape(4, 4, *packed[2:]).swapaxes(0, 1)
    line = summed([grid[0], *(grid[k].astype(BF16) for k in (1, 2, 3))], "dom", 1)
    cell = summed(line, "dom", 4)
    cell = after(cell, *returned[1:])
    cell = cell + swapped(cell, "rep", 2)
    cell = cell + swapped(cell, "dom", 16)
    total = (cell + swapped(cell, "dom", 32)).astype(BF16)
    src_sum = src_keep + swapped(src_send, "rep", 1).astype(F32)
    src_got = swapped(after(src_sum[1], total).astype(BF16), "rep", 2)
    line = collected(total, "dom", 4)
    grid = after(collected(line, "dom", 1), src_got)
    grid_core = swapped(grid, "rep", 1)

    kept = src_sum[0] + src_got.astype(F32)
    grads = kept + jnp.concatenate(returned, axis=1).astype(F32)

    new_state = entity_state + jnp.mean(grads * grads, axis=0)
    new_slab = (own.astype(F32) - RATE * grads / jnp.sqrt(new_state)[None, :]).astype(BF16)
    new_relation, new_relation_state = call(
        relation_update_kernel,
        "relation_update",
        1,
        [whole((width, n_rel)), whole((1, n_rel))] + [whole(grid.shape)] * 2,
        [whole((width, n_rel)), whole((1, n_rel))],
        [f32_of(width, n_rel), f32_of(1, n_rel)],
        [pltpu.VMEM(packed, F32)],
        fixed,
        relations,
        relation_state.reshape(1, n_rel),
        grid,
        grid_core,
    )
    return (new_slab.T, new_state, new_relation.T, new_relation_state.reshape(n_rel))


def solution(mesh):
    in_specs = (
        P("dom", None),
        P(("dom", "rep")),
        P(),
        P(),
        P(("dom", "rep")),
        P(("dom", "rep")),
        P(("dom", "rep")),
        P(("dom", "rep")),
        P("dom"),
    )
    out_specs = (P(("dom", "rep"), None), P(("dom", "rep")), P(), P())
    return jax.shard_map(body, mesh=mesh, in_specs=in_specs, out_specs=out_specs, check_vma=False)
```

```python
import functools

import jax
import jax.numpy as jnp
from jax import lax
from jax.experimental import pallas as pl
from jax.experimental.pallas import tpu as pltpu
from jax.sharding import PartitionSpec as P

BLOCK = 512
FINE = 256
WIDE = 1024
WINDOW = 1280
LANES = 128
SUBLANES = 8
PIECES = 2
VMEM_BYTES = 56 << 20
RATE = 0.1
BF16, F32, I32 = jnp.bfloat16, jnp.float32, jnp.int32


def swapped(x, axis, mask):
    return lax.ppermute(x, axis, [(i, i ^ mask) for i in range(lax.axis_size(axis))])


def swapped_far(x, dom_mask, rep_mask):
    doms, reps = lax.axis_size("dom"), lax.axis_size("rep")
    pairs = [
        (d * reps + r, (d ^ dom_mask) * reps + (r ^ rep_mask))
        for d in range(doms)
        for r in range(reps)
    ]
    return lax.ppermute(x, ("dom", "rep"), pairs)


def one_hot(idx, base, rows):
    row = lax.broadcasted_iota(I32, (rows, idx.shape[1]), 0)
    return jnp.where(row == idx - base, 1.0, 0.0).astype(BF16)


def mm(a, b):
    return jnp.dot(a, b, preferred_element_type=F32)


def mm_nt(a, b):
    return lax.dot_general(a, b, (((1,), (1,)), ((), ())), preferred_element_type=F32)


def call(kernel, name, grid, in_specs, out_specs, out_shape, scratch, *args, flops=0):
    return pl.pallas_call(
        kernel,
        grid_spec=pltpu.PrefetchScalarGridSpec(
            num_scalar_prefetch=1,
            grid=(grid,),
            in_specs=in_specs,
            out_specs=out_specs,
            scratch_shapes=scratch,
        ),
        out_shape=out_shape,
        compiler_params=pltpu.CompilerParams(vmem_limit_bytes=VMEM_BYTES),
        cost_estimate=pl.CostEstimate(flops=flops, bytes_accessed=0, transcendentals=0),
        name=name,
    )(*args)


def whole(shape):
    return pl.BlockSpec(shape, lambda i, c: (0,) * len(shape))


def edge_block(rows, block=BLOCK):
    return pl.BlockSpec((rows, block), lambda i, c: (0, i))


def live(scal, block=BLOCK):
    return pl.program_id(0) * block < scal[0]


def span(scal, which, block):
    each = block // FINE
    at = 3 + which
    first, last = None, None
    for k in range(each):
        cell = at + 4 * (pl.program_id(0) * each + k)
        low, high = scal[cell], scal[cell + 1]
        first = low if first is None else jnp.minimum(first, low)
        last = high if last is None else jnp.maximum(last, high)
    return first, last


def meets(spanned, base, rows):
    return (spanned[0] < base + rows) & (spanned[1] >= base)


def table_rows(idx, pieces):
    total = None
    for base, piece in pieces:
        y = mm(piece, one_hot(idx, base, piece.shape[1]))
        total = y if total is None else total + y
    return total


def over_windows(scal, rows, idx_ref, visit):
    cells = []
    for k in range(WIDE // FINE):
        at = 3 + 4 * (pl.program_id(0) * (WIDE // FINE) + k)
        low, high = scal[at], scal[at + 1]
        base = jnp.minimum(low // LANES * LANES, rows - WINDOW)
        cells.append((slice(k * FINE, (k + 1) * FINE), base, high))

    def one(lanes, base, w):
        low = base + w * WINDOW
        first = pl.multiple_of(jnp.minimum(low, rows - WINDOW), LANES)
        idx = idx_ref[:, lanes]
        idx = jnp.where(idx >= low, idx - first, -1)
        visit(lanes, pl.ds(first, WINDOW), one_hot(idx, 0, WINDOW))

    for lanes, base, _ in cells:
        one(lanes, base, 0)
    for lanes, base, high in cells:

        @pl.when(high >= base + WINDOW)
        def _():
            turns = (high - base) // WINDOW + 1
            lax.fori_loop(1, turns, lambda w, _: one(lanes, base, w), None)


def gather_kernel(scal, idx_ref, table_ref, out_ref, acc):
    @pl.when(live(scal, WIDE))
    def _():
        acc[...] = jnp.zeros_like(acc)

        def visit(lanes, rows, hot):
            acc[:, lanes] += mm(table_ref[:, rows], hot)

        over_windows(scal, table_ref.shape[1], idx_ref, visit)
        out_ref[...] = acc[...].astype(out_ref.dtype)


def negatives_kernel(scal, idx_ref, table_ref, out_ref):
    rows, chunk = table_ref.shape[1], 1024
    pieces = [(b, table_ref[:, b : b + chunk]) for b in range(0, rows, chunk)]
    out_ref[...] = table_rows(idx_ref[...], pieces).astype(out_ref.dtype)


def relation_gather_kernel(scal, idx_ref, table_ref, out_ref):
    @pl.when(live(scal))
    def _():
        both = table_rows(idx_ref[...], [(0, table_ref[...])])
        half = both.shape[0] // 2
        out_ref[...] = both[:half] + both[half:]


def valid_lanes(scal):
    lane = lax.broadcasted_iota(I32, (1, BLOCK), 1) + pl.program_id(0) * BLOCK
    return jnp.where(lane < scal[0], 1.0, 0.0)


def negative_scores_kernel(scal, s_ref, r_ref, neg_t_ref, half_neg_ref, gu_ref, gn_ref, acc):
    i = pl.program_id(0)

    @pl.when(i == 0)
    def _():
        acc[...] = jnp.zeros_like(acc)

    @pl.when(live(scal))
    def _():
        ub = (s_ref[...].astype(F32) * r_ref[...]).astype(BF16)
        half = mm(half_neg_ref[...], ub)
        weight = valid_lanes(scal) * (0.5 / half.shape[0])
        gneg = (jnp.tanh(half) * weight + weight).astype(BF16)
        gu_ref[...] = mm(neg_t_ref[...], gneg)
        acc[...] += mm_nt(ub, gneg)

    @pl.when(i == pl.num_programs(0) - 1)
    def _():
        gn_ref[...] = acc[...].astype(BF16)


def target_kernel(order, rows, scal, s_ref, r_ref, gun_ref, idx_ref, *refs):
    gn_ref, n_idx_ref, tables = refs[0], refs[1], refs[2 : 2 + len(order)]
    gs_ref, gr_ref, *keep_refs = refs[2 + len(order) : 6 + len(order)]
    *send_refs, t_acc, gt_scr, acc = refs[6 + len(order) :]
    i = pl.program_id(0)
    parts = 2 * acc.shape[0]
    sums = [acc.at[k // 2] if k % 2 else keep_refs[k // 2] for k in range(parts)]
    bases = [(scal[1] ^ apart) * rows for apart in range(parts)]

    @pl.when(i == 0)
    def _():
        for total, base in zip(sums, bases, strict=True):
            total[...] = mm_nt(gn_ref[...], one_hot(n_idx_ref[...], base, rows))

    @pl.when(live(scal))
    def _():
        spanned = span(scal, 2, BLOCK)
        t_acc[...] = jnp.zeros_like(t_acc)
        for apart, base in enumerate(bases):

            @pl.when(meets(spanned, base, rows))
            def _():
                pieces = [
                    (base + first, table[...])
                    for (k, first), table in zip(order, tables, strict=True)
                    if k == apart
                ]
                t_acc[...] += table_rows(idx_ref[...], pieces)

        t = t_acc[...]
        s = s_ref[...].astype(F32)
        r = r_ref[...]
        u = s * r
        pos = jnp.sum(u * t, axis=0, keepdims=True)
        gpos = -jax.nn.sigmoid(-pos) * valid_lanes(scal)
        gu = gpos * t + gun_ref[...]
        gs_ref[...] = (gu * r).astype(BF16)
        gr_ref[...] = (gu * s).astype(BF16)
        gt_scr[...] = (gpos * u).astype(BF16)
        for total, base in zip(sums, bases, strict=True):

            @pl.when(meets(spanned, base, rows))
            def _():
                total[...] += mm_nt(gt_scr[...], one_hot(idx_ref[...], base, rows))

    @pl.when(jnp.logical_not(live(scal)))
    def _():
        gs_ref[...] = jnp.zeros_like(gs_ref)
        gr_ref[...] = jnp.zeros_like(gr_ref)

    @pl.when(i == pl.num_programs(0) - 1)
    def _():
        for k, send_ref in enumerate(send_refs):
            send_ref[...] = acc[k].astype(BF16)


def relation_scatter_kernel(scal, g_ref, idx_ref, keep_ref, send_ref, acc):
    i = pl.program_id(0)

    @pl.when(i == 0)
    def _():
        acc[...] = jnp.zeros_like(acc)

    @pl.when(live(scal, WIDE))
    def _():
        acc[...] += mm_nt(g_ref[...], one_hot(idx_ref[...], 0, acc.shape[1]))

    def copy(core):
        for part, cell, slot, rows, cols in tiles((2, *keep_ref.shape), acc.shape):
            to = (keep_ref, send_ref)[part ^ core]
            at = (cell ^ (scal[2] & 15), pl.ds(slot * SUBLANES, SUBLANES))
            if rows is None:
                to[at] = jnp.zeros((SUBLANES, LANES), F32)
            else:
                to[at] = acc[rows, cols]

    for core in range(2):

        @pl.when((i == pl.num_programs(0) - 1) & (scal[1] & 1 == core))
        def _():
            copy(core)


def tiles(packed, flat):
    parts, cells, rows, _ = packed
    slots = rows // SUBLANES
    wide = flat[1] // parts // LANES
    for part in range(parts):
        for tile in range(cells * slots):
            cell, slot = divmod(tile, slots)
            row, col = divmod(tile, wide)
            if row * SUBLANES >= flat[0]:
                yield part, cell, slot, None, None
            else:
                row, col = row * SUBLANES, (part * wide + col) * LANES
                yield part, cell, slot, slice(row, row + SUBLANES), slice(col, col + LANES)


def scatter_kernel(scal, g_ref, idx_ref, keep_ref, send_ref, acc):
    i = pl.program_id(0)

    @pl.when(i == 0)
    def _():
        acc[...] = jnp.zeros_like(acc)

    @pl.when(live(scal, WIDE))
    def _():
        def visit(lanes, rows, hot):
            acc[:, rows] += mm_nt(g_ref[:, lanes], hot)

        over_windows(scal, acc.shape[1], idx_ref, visit)

    @pl.when(i == pl.num_programs(0) - 1)
    def _():
        rows = keep_ref.shape[2]
        for apart in range(acc.shape[1] // rows):
            part = acc[:, pl.ds(pl.multiple_of((scal[1] ^ apart) * rows, rows), rows)]
            to = (keep_ref, send_ref)[apart % 2]
            to[apart // 2] = part.astype(to.dtype)


def relation_update_kernel(scal, rel_ref, state_ref, near_ref, core_ref, *refs):
    new_rel_ref, new_state_ref, flat = refs
    parts, cells, rows, _ = flat.shape
    for k, g_ref in enumerate((near_ref, core_ref)):
        for cell in range(cells):
            away = cell ^ (scal[2] & 15)
            flat[(scal[1] & 1) ^ k, cell] = g_ref[away & 3, away >> 2].astype(F32)
    width, count = rel_ref.shape
    wide = -(-count // (parts * LANES)) * parts * LANES
    pieces = {}
    for part, cell, slot, trows, tcols in tiles(flat.shape, (width, wide)):
        if trows is not None:
            pieces[trows.start, tcols.start] = (part, cell, pl.ds(slot * SUBLANES, SUBLANES))
    for col in range(0, count, LANES):
        n = min(LANES, count - col)
        square = jnp.zeros((SUBLANES, LANES), F32)
        for row in range(0, width, SUBLANES):
            g = flat[pieces[row, col]]
            square = square + g * g
        mean = jnp.sum(square, axis=0, keepdims=True) * (1.0 / width)
        state = state_ref[:, col : col + n] + mean[:, :n]
        new_state_ref[:, col : col + n] = state
        scale = RATE / jnp.sqrt(state)
        for row in range(0, width, SUBLANES):
            at = (slice(row, row + SUBLANES), slice(col, col + n))
            new_rel_ref[at] = rel_ref[at] - flat[pieces[row, col]][:, :n] * scale


def after(x, *others):
    return lax.optimization_barrier((x, *others))[0]


def summed(x, axis, step):
    got = [swapped(x[k], axis, k * step).astype(F32) for k in (1, 2, 3)]
    return (x[0] + got[0]) + (got[1] + got[2])


def collected(x, axis, step):
    return jnp.stack([x] + [swapped(x, axis, k * step) for k in (1, 2, 3)])


def body(
    entity_slab,
    entity_state,
    relation_diag,
    relation_state,
    edge_source,
    edge_target,
    edge_relation,
    edge_count,
    negatives,
):
    slab = entity_slab.T
    relations = relation_diag.T
    width, rows_part = slab.shape
    reps = lax.axis_size("rep")
    half = lax.axis_size("dom") // 2
    quarter = rows_part // reps
    rep, dom = lax.axis_index("rep"), lax.axis_index("dom")
    edges, n_neg, n_rel = edge_source.shape[0], negatives.shape[0], relation_diag.shape[0]
    f32_of = lambda *shape: jax.ShapeDtypeStruct(shape, F32)
    bf16_of = lambda *shape: jax.ShapeDtypeStruct(shape, BF16)

    asked = swapped(negatives, "dom", half).reshape(1, n_neg)
    own = lax.dynamic_slice_in_dim(slab, rep * quarter, quarter, 1)
    step = quarter // PIECES
    own_pieces = [own[:, k * step : (k + 1) * step] for k in range(PIECES)]

    lane = jnp.arange(edges, dtype=I32)
    is_live = lane < edge_count[0]
    group = edge_target // quarter
    along = jnp.where(group % 2 == 0, edge_source, rows_part - 1 - edge_source)
    key = jnp.where(is_live, group * rows_part + along, reps * rows_part)
    _, src, dst, rel = lax.sort((key, edge_source, edge_target, edge_relation), num_keys=1)
    spans = []
    for idx in (src, dst):
        by_cell = idx.reshape(-1, FINE)
        cell_live = is_live.reshape(-1, FINE)
        spans.append(jnp.min(jnp.where(cell_live, by_cell, rows_part), axis=1))
        spans.append(jnp.max(jnp.where(cell_live, by_cell, -1), axis=1))
    fixed = jnp.stack([edge_count[0], rep.astype(I32), dom.astype(I32)])
    scal = jnp.concatenate([fixed, jnp.stack(spans, axis=1).reshape(-1)])
    src, dst, rel = (x.reshape(1, edges) for x in (src, dst, rel))

    quarter_neg = n_neg // reps
    found = call(
        negatives_kernel,
        "partner_negatives",
        1,
        [whole((1, quarter_neg)), whole(slab.shape)],
        whole((width, quarter_neg)),
        bf16_of(width, quarter_neg),
        [],
        fixed,
        lax.dynamic_slice_in_dim(asked, rep * quarter_neg, quarter_neg, 1),
        slab,
    )
    neg_far = swapped_far(found, half, 2)
    own_pieces[1:] = [after(x, found) for x in own_pieces[1:]]
    far = [swapped_far(x, half, 2) for x in own_pieces]
    s_rows = call(
        gather_kernel,
        "source_rows",
        edges // WIDE,
        [edge_block(1, WIDE), whole(slab.shape)],
        edge_block(width, WIDE),
        bf16_of(width, edges),
        [pltpu.VMEM((width, WIDE), F32)],
        scal,
        after(src, found),
        slab,
    )
    wide = -(-n_rel // (2 * LANES)) * 2 * LANES
    padded = jnp.pad(relations, ((0, 0), (0, wide - n_rel)))
    high = padded.astype(BF16)
    low = (padded - high.astype(F32)).astype(BF16)
    split = jnp.concatenate([high, low], axis=0)
    split = after(split, s_rows)
    r_rows = call(
        relation_gather_kernel,
        "relation_rows",
        edges // BLOCK,
        [edge_block(1), whole(split.shape)],
        edge_block(width),
        f32_of(width, edges),
        [],
        scal,
        rel,
        split,
    )
    neg_far = after(neg_far, split)
    neg_near = swapped(neg_far, "rep", 2)
    neg_far_core = swapped(neg_far, "rep", 1)
    neg_near = after(neg_near, r_rows)
    neg_near_core = swapped(neg_near, "rep", 1)
    neg_t = jnp.concatenate([neg_far, neg_near, neg_far_core, neg_near_core], axis=1)
    apart_by = (2, 0, 3, 1)
    neg_idx = jnp.concatenate(
        [
            lax.dynamic_slice_in_dim(negatives, (rep ^ k) * quarter_neg, quarter_neg, 0)
            for k in apart_by
        ]
    ).reshape(1, n_neg)
    half_neg = 0.5 * neg_t.T
    far = [after(x, r_rows) for x in far]
    near = [swapped(x, "rep", 2) for x in far]
    far_core = [swapped(x, "rep", 1) for x in far]
    gu_neg, grad_n = call(
        negative_scores_kernel,
        "negative_scores",
        edges // BLOCK,
        [edge_block(width), edge_block(width), whole((width, n_neg)), whole((n_neg, width))],
        [edge_block(width), whole((width, n_neg))],
        [f32_of(width, edges), bf16_of(width, n_neg)],
        [pltpu.VMEM((width, n_neg), F32)],
        scal,
        s_rows,
        r_rows,
        after(neg_t, *far),
        half_neg,
    )
    near = [after(x, gu_neg) for x in near]
    near_core = [swapped(x, "rep", 1) for x in near]
    tables = [*far, *near, *far_core, *near_core]
    order = tuple((k, piece * step) for k in apart_by for piece in range(PIECES))

    cells = 16
    slots = -(-(width // SUBLANES * wide // 2 // LANES) // cells)
    packed = (2, cells, slots * SUBLANES, LANES)
    half_parts = (reps // 2, width, quarter)
    part = (width, quarter)
    grad_s, grad_r, keep_on, keep_back, send_on, send_back = call(
        functools.partial(target_kernel, order, quarter),
        "targets",
        edges // BLOCK,
        [edge_block(width)] * 3
        + [edge_block(1)]
        + [whole((width, n_neg)), whole((1, n_neg))]
        + [whole(t.shape) for t in tables],
        [edge_block(width)] * 2 + [whole(part)] * 4,
        [bf16_of(width, edges)] * 2 + [f32_of(*part)] * 2 + [bf16_of(*part)] * 2,
        [
            pltpu.VMEM((width, BLOCK), F32),
            pltpu.VMEM((width, BLOCK), BF16),
            pltpu.VMEM(half_parts, F32),
        ],
        scal,
        s_rows,
        r_rows,
        gu_neg,
        dst,
        grad_n,
        neg_idx,
        *tables,
    )
    on = (keep_on + swapped(send_on, "rep", 1).astype(F32)).astype(BF16)
    sent = [swapped(on[:, k * step : (k + 1) * step], "rep", 2) for k in range(PIECES)]
    rel_keep, rel_send = call(
        relation_scatter_kernel,
        "relation_grads",
        edges // WIDE,
        [edge_block(width, WIDE), edge_block(1, WIDE)],
        [whole(packed[1:])] * 2,
        [f32_of(*packed[1:])] * 2,
        [pltpu.VMEM((width, wide), F32)],
        scal,
        after(grad_r, on),
        rel,
        flops=2 * width * wide * edges,
    )
    back = keep_back + after(swapped(send_back, "rep", 1), rel_keep).astype(F32)
    first = back[:, :step] + after(sent[0], rel_keep).astype(F32)
    first = first.astype(BF16)
    returned = [swapped_far(first, half, 2)]
    src_keep, src_send = call(
        scatter_kernel,
        "source_grads",
        edges // WIDE,
        [edge_block(width, WIDE), edge_block(1, WIDE)],
        [whole(half_parts)] * 2,
        [f32_of(*half_parts), bf16_of(*half_parts)],
        [pltpu.VMEM((width, rows_part), F32)],
        scal,
        after(grad_s, first),
        src,
        flops=width * rows_part * edges,
    )

    last = back[:, step:] + after(sent[1], src_keep).astype(F32)
    last = last.astype(BF16)
    returned.append(swapped_far(last, half, 2))

    grid = rel_keep + after(swapped(rel_send, "rep", 1), src_keep, returned[0], last)
    grid = grid.reshape(4, 4, *packed[2:]).swapaxes(0, 1)
    line = summed([grid[0], *(grid[k].astype(BF16) for k in (1, 2, 3))], "dom", 1)
    cell = summed(line, "dom", 4)
    cell = after(cell, *returned[1:])
    cell = cell + swapped(cell, "rep", 2)
    total = summed([cell] * 4, "dom", 16).astype(BF16)
    src_sum = src_keep + swapped(src_send, "rep", 1).astype(F32)
    src_got = swapped(after(src_sum[1], total).astype(BF16), "rep", 2)
    line = collected(total, "dom", 4)
    grid = after(collected(line, "dom", 1), src_got)
    grid_core = swapped(grid, "rep", 1)

    kept = src_sum[0] + src_got.astype(F32)
    grads = kept + jnp.concatenate(returned, axis=1).astype(F32)

    new_state = entity_state + jnp.mean(grads * grads, axis=0)
    new_slab = (own.astype(F32) - RATE * grads / jnp.sqrt(new_state)[None, :]).astype(BF16)
    new_relation, new_relation_state = call(
        relation_update_kernel,
        "relation_update",
        1,
        [whole((width, n_rel)), whole((1, n_rel))] + [whole(grid.shape)] * 2,
        [whole((width, n_rel)), whole((1, n_rel))],
        [f32_of(width, n_rel), f32_of(1, n_rel)],
        [pltpu.VMEM(packed, F32)],
        fixed,
        relations,
        relation_state.reshape(1, n_rel),
        grid,
        grid_core,
    )
    return (new_slab.T, new_state, new_relation.T, new_relation_state.reshape(n_rel))


def solution(mesh):
    in_specs = (
        P("dom", None),
        P(("dom", "rep")),
        P(),
        P(),
        P(("dom", "rep")),
        P(("dom", "rep")),
        P(("dom", "rep")),
        P(("dom", "rep")),
        P("dom"),
    )
    out_specs = (P(("dom", "rep"), None), P(("dom", "rep")), P(), P())
    return jax.shard_map(body, mesh=mesh, in_specs=in_specs, out_specs=out_specs, check_vma=False)
```
